256 devices in a mesh: dp: 32 (over x, z), seq: 8 (over y, core).
Axes of the slice: x: 4, y: 4, z: 8, core: 2. Of those that a mesh axis runs over, the one named last changes fastest.
Arguments:
- normed_block_input: bfloat16 [32, 1024, 8192], P('dp', 'seq'), may hold values from -6 to 6
- saved_queries: bfloat16 [32, 1024, 4096], P('dp', 'seq'), may hold values from -40 to 40
- saved_keys: bfloat16 [32, 1024, 512], P('dp', 'seq'), may hold values from -6 to 6
- saved_values: bfloat16 [32, 1024, 512], P('dp', 'seq'), may hold values from -6 to 6
- attention_output: bfloat16 [32, 1024, 4096], P('dp', 'seq'), may hold values from -6 to 6
- output_gradient: bfloat16 [32, 1024, 4096], P('dp', 'seq'), may hold values from -6 to 6
- adapter_down_weight: bfloat16 [8192, 192], replicated, may hold values from -0.0625 to 0.0625
- query_up_weight: bfloat16 [64, 4096], replicated, may hold values from -0.75 to 0.75
- key_up_weight: bfloat16 [64, 512], replicated, may hold values from -0.75 to 0.75
- value_up_weight: bfloat16 [64, 512], replicated, may hold values from -0.75 to 0.75
Outputs:
- query_gradient: bfloat16 [32, 1024, 4096], P('dp', 'seq')
- key_gradient: bfloat16 [32, 1024, 512], P('dp', 'seq')
- value_gradient: bfloat16 [32, 1024, 512], P('dp', 'seq')
- down_grad: float32 [8192, 192], P(('dp', 'seq'))
- up_grad_q: float32 [64, 4096], replicated
- up_grad_k: float32 [64, 512], replicated
- up_grad_v: float32 [64, 512], replicated
The draws below stay inside these ranges and needn't reach their ends.
All inputs are finite; a program needn't handle non-finite values.
Results may differ from the reference program's by a relative error of at most 0.0065.
Values may be sent and summed in bfloat16 or wider, within the bound.
A program may use at most 128 MiB of HBM per device.

```python
import math
import jax
import jax.numpy as jnp
from jax import lax

MODEL_WIDTH = 8192
QUERY_HEAD_COUNT = 32
KEY_VALUE_HEADS = 4
HEAD_SIZE = 128
ADAPTER_RANK = 64
SLAB_LENGTH = 1024
SLAB_COUNT = 32
N_SEQ = 8


def base_keys(key):
    return jnp.clip(jax.random.normal(key, (SLAB_COUNT, SLAB_LENGTH, KEY_VALUE_HEADS * HEAD_SIZE), jnp.float32), -6.0, 6.0)


def draw_saved_keys(key, part):
    every_key = base_keys(key)
    return every_key.astype(jnp.bfloat16)


def draw_saved_queries(key, part):
    key = jax.random.fold_in(key, 11)
    values = jnp.clip(jax.random.normal(key, (SLAB_COUNT, SLAB_LENGTH, QUERY_HEAD_COUNT * HEAD_SIZE), jnp.float32), -6.0, 6.0)
    return values.astype(jnp.bfloat16)


def spiked(result, rng, source, target, blocks, factor):
    owner, partner = [(jnp.arange(result.shape[axis_at]) // (result.shape[axis_at] // blocks)).reshape([-1 if axis == axis_at else 1 for axis in range(result.ndim)]) for axis_at in (source, target)]
    chosen = jax.random.permutation(rng, blocks)[partner]
    strong = (owner == chosen) | (owner == (partner + blocks // 2) % blocks)
    return jnp.where(strong, factor * result, result)


def shard_levels(own_key, shape, split, least, largest):
    level = 1.0
    for position, blocks in split:
        steps = jax.random.uniform(jax.random.fold_in(jax.random.fold_in(own_key, 6), position), (blocks,), jnp.float32, least / len(split), largest / len(split))
        level = level * jnp.repeat(jnp.exp(steps), shape[position] // blocks).reshape((-1,) + (1,) * (len(shape) - 1 - position))
    return level


def bell_draw(rng, shape, scale, bound, pieces=(), dtype=jnp.bfloat16):
    gain = shard_levels(rng, shape, pieces, -0.22, 0.18) if pieces else 1.0
    array = jax.random.normal(rng, shape, jnp.float32) * scale * gain
    return jnp.minimum(jnp.maximum(array, -bound), bound).astype(dtype)


def noise_with(key, extent, scale, most, cuts, heavy, held_as=jnp.bfloat16):
    array = scale * jax.random.normal(key, extent, jnp.float32)
    if cuts:
        array = array * shard_levels(key, extent, cuts, -0.22, 0.18)
    return jnp.clip(spiked(array, jax.random.fold_in(key, 3), *heavy), -most, most).astype(held_as)


def setup_inputs(seed: int = 0) -> dict:
    streams_of = jax.random.split(jax.random.key(seed), 11)
    return {
        "normed_block_input": noise_with(streams_of[0], (SLAB_COUNT, SLAB_LENGTH, MODEL_WIDTH), 1.0, 6.0, ((0, 32), (1, 8)), (0, 2, 32, 2.75)),
        "saved_queries": draw_saved_queries(jax.random.fold_in(streams_of[10], 71), 0),
        "saved_keys": draw_saved_keys(jax.random.fold_in(streams_of[10], 71), 0),
        "saved_values": bell_draw(streams_of[3], (SLAB_COUNT, SLAB_LENGTH, KEY_VALUE_HEADS * HEAD_SIZE), 1.0, 6.0, ((0, 32), (1, 8))),
        "attention_output": bell_draw(streams_of[4], (SLAB_COUNT, SLAB_LENGTH, QUERY_HEAD_COUNT * HEAD_SIZE), 1.0, 6.0, ((0, 32), (1, 8))),
        "output_gradient": bell_draw(streams_of[5], (SLAB_COUNT, SLAB_LENGTH, QUERY_HEAD_COUNT * HEAD_SIZE), 1.0, 6.0, ((0, 32), (1, 8))),
        "adapter_down_weight": bell_draw(streams_of[6], (MODEL_WIDTH, 3 * ADAPTER_RANK), MODEL_WIDTH ** -0.5, 0.0625),
        "query_up_weight": bell_draw(streams_of[7], (ADAPTER_RANK, QUERY_HEAD_COUNT * HEAD_SIZE), ADAPTER_RANK ** -0.5, 0.75),
        "key_up_weight": bell_draw(streams_of[8], (ADAPTER_RANK, KEY_VALUE_HEADS * HEAD_SIZE), ADAPTER_RANK ** -0.5, 0.75),
        "value_up_weight": bell_draw(streams_of[9], (ADAPTER_RANK, KEY_VALUE_HEADS * HEAD_SIZE), ADAPTER_RANK ** -0.5, 0.75),
    }


ADAPTER_SCALE = 0.25

def slab_back(arrays):
    query_slab, slab_keys, slab_values, output_slab, grad_slab = arrays
    span_length = query_slab.shape[0]
    repeat_factor = max(1, N_SEQ // KEY_VALUE_HEADS)
    runs_total = KEY_VALUE_HEADS * repeat_factor
    group_size = QUERY_HEAD_COUNT // runs_total
    score_scale = HEAD_SIZE ** (-0.5)
    queries = query_slab.reshape(span_length, runs_total, group_size, HEAD_SIZE).astype(jnp.float32)
    grads = grad_slab.reshape(span_length, runs_total, group_size, HEAD_SIZE).astype(jnp.float32)
    outputs = output_slab.reshape(span_length, runs_total, group_size, HEAD_SIZE).astype(jnp.float32)
    deltas = lax.optimization_barrier(jnp.sum(grads * outputs, axis=-1))
    every_key = jnp.repeat(slab_keys.reshape(span_length, KEY_VALUE_HEADS, HEAD_SIZE), repeat_factor, axis=1).astype(jnp.float32)
    every_value = jnp.repeat(slab_values.reshape(span_length, KEY_VALUE_HEADS, HEAD_SIZE), repeat_factor, axis=1).astype(jnp.float32)
    scores = jnp.einsum('qrgd,srd->rgqs', queries, every_key) * score_scale
    positions = jnp.arange(span_length)
    visible = positions[None, :] <= positions[:, None]
    scores = jnp.where(visible, scores, -jnp.inf)
    row_max = lax.optimization_barrier(jnp.max(scores, axis=-1, keepdims=True))
    weights = jnp.exp(scores - row_max)
    probability = weights / lax.optimization_barrier(jnp.sum(weights, axis=-1, keepdims=True))
    probs_low = lax.optimization_barrier(probability.astype(jnp.bfloat16)).astype(jnp.float32)
    value_run_list = jnp.einsum('rgqs,qrgd->srd', probs_low, grads)
    prob_grad = jnp.einsum('qrgd,srd->rgqs', grads, every_value)
    score_grad = probability * (prob_grad - jnp.transpose(deltas, (1, 2, 0))[..., None])
    score_low = lax.optimization_barrier(score_grad.astype(jnp.bfloat16)).astype(jnp.float32)
    query_gradient = (jnp.einsum('rgqs,srd->qrgd', score_low, every_key) * score_scale).astype(jnp.bfloat16)
    key_run_list = (jnp.einsum('rgqs,qrgd->srd', score_low, queries) * score_scale).astype(jnp.bfloat16)
    value_run_list = value_run_list.astype(jnp.bfloat16)
    key_run_list = lax.optimization_barrier(key_run_list).astype(jnp.float32)
    value_run_list = lax.optimization_barrier(value_run_list).astype(jnp.float32)
    key_gradient = lax.optimization_barrier(jnp.sum(key_run_list.reshape(span_length, KEY_VALUE_HEADS, repeat_factor, HEAD_SIZE), axis=2)).astype(jnp.bfloat16)
    value_gradient = lax.optimization_barrier(jnp.sum(value_run_list.reshape(span_length, KEY_VALUE_HEADS, repeat_factor, HEAD_SIZE), axis=2)).astype(jnp.bfloat16)
    return (query_gradient.reshape(span_length, QUERY_HEAD_COUNT * HEAD_SIZE), key_gradient.reshape(span_length, KEY_VALUE_HEADS * HEAD_SIZE), value_gradient.reshape(span_length, KEY_VALUE_HEADS * HEAD_SIZE))

def reference(normed_block_input, saved_queries, saved_keys, saved_values, attention_output, output_gradient, adapter_down_weight, query_up_weight, key_up_weight, value_up_weight):
    query_gradient, key_gradient, value_gradient = lax.map(slab_back, (saved_queries, saved_keys, saved_values, attention_output, output_gradient))
    flattened_input = normed_block_input.reshape(-1, MODEL_WIDTH)
    flattened_queries = query_gradient.reshape(-1, QUERY_HEAD_COUNT * HEAD_SIZE)
    flattened_keys = key_gradient.reshape(-1, KEY_VALUE_HEADS * HEAD_SIZE)
    flattened_values = value_gradient.reshape(-1, KEY_VALUE_HEADS * HEAD_SIZE)
    down_activation = jnp.dot(flattened_input, adapter_down_weight, preferred_element_type=jnp.float32).astype(jnp.bfloat16)
    multiplier = ADAPTER_SCALE / math.sqrt(SLAB_COUNT * SLAB_LENGTH)
    up_grad_q = multiplier * jnp.dot(down_activation[:, :ADAPTER_RANK].T, flattened_queries, preferred_element_type=jnp.float32)
    up_grad_k = multiplier * jnp.dot(down_activation[:, ADAPTER_RANK:2 * ADAPTER_RANK].T, flattened_keys, preferred_element_type=jnp.float32)
    up_grad_v = multiplier * jnp.dot(down_activation[:, 2 * ADAPTER_RANK:].T, flattened_values, preferred_element_type=jnp.float32)
    middle_term = jnp.concatenate([jnp.dot(flattened_queries, query_up_weight.T, preferred_element_type=jnp.float32), jnp.dot(flattened_keys, key_up_weight.T, preferred_element_type=jnp.float32), jnp.dot(flattened_values, value_up_weight.T, preferred_element_type=jnp.float32)], axis=1).astype(jnp.bfloat16)
    down_grad = multiplier * jnp.dot(flattened_input.T, middle_term, preferred_element_type=jnp.float32)
    return (query_gradient, key_gradient, value_gradient, down_grad, up_grad_q, up_grad_k, up_grad_v)
```

```python
import math

import jax
import jax.numpy as jnp
from jax import lax
from jax.experimental import pallas as pl
from jax.experimental.pallas import tpu as pltpu
from jax.sharding import PartitionSpec as P

BF = jnp.bfloat16
F32 = jnp.float32
HEAD = 128
SCALE = HEAD**-0.5
LOG2_SCALE = SCALE * math.log2(math.e)
FACTOR = 0.25 / math.sqrt(32768)
NX, NY, NZ = 4, 4, 8
PAIR = 512


def dot(left, right, left_axis, right_axis):
    return lax.dot_general(
        left, right, (((left_axis,), (right_axis,)), ((), ())), preferred_element_type=F32
    )


def kernel(
    x_in, q_in, k_in, v_in, o_in, g_in, wd_in, wq_in, wk_in, wv_in,
    dq_out, dk_out, dv_out, down_out, upq_out, upk_out, upv_out,
    xv, wd, wq, wk, wv, qb, gb, kb, vb, gown, oown, deltas, down_act,
    xcols, scores, row_max, dq_acc, dq_rows, grads_out, grads_in, own_grads,
    kv_rows, mid_part, mid_sib, mid_all, down_part, down_y, down_z, down_zin,
    up_part, up_x, up_xsum, up_z, up_piece, up_y, up_final, up_slab, up_all,
    loc, sib_s, sib_r, kv_s, kv_r, x_s, x_r, gr_s, gr_r, mid_s, mid_r,
    dy_s, dy_r, dz_s, dz_r, ux_s, ux_r, uz_s, uz_r, uy_s, uy_r, az_s, az_r, ax_s, ax_r,
):
    dp = lax.axis_index("dp")
    seq = lax.axis_index("seq")
    x, z = dp // NZ, dp % NZ
    y, c = seq // 2, seq % 2
    oc = 1 - c

    def at(xx, yy, zz, cc):
        return {"dp": xx * NZ + zz, "seq": yy * 2 + cc}

    sibling = at(x, y, z, oc)

    def remote(src, dst, ssem, rsem, device):
        return pltpu.make_async_remote_copy(
            src_ref=src, dst_ref=dst, send_sem=ssem, recv_sem=rsem,
            device_id=device, device_id_type=pl.DeviceIdType.MESH,
        )

    def arrived(dst, rsem, ssem):
        remote(dst, dst, ssem, rsem, sibling).wait_recv()

    def part(start, size, unit):
        return pl.ds(pl.multiple_of(start * unit, unit), size)

    locals_ = []

    def local(src, dst, index):
        copy = pltpu.make_async_copy(src, dst, loc.at[index])
        copy.start()
        locals_.append(copy)
        return copy

    my_rows = part(c, 128, 128)
    c_gown = local(g_in.at[0], gown, 0)
    c_oown = local(o_in.at[0], oown, 1)
    c_q = local(q_in.at[0, :, part(c, 2048, 2048)], qb.at[my_rows], 2)
    c_g = local(g_in.at[0, :, part(c, 2048, 2048)], gb.at[my_rows], 3)
    chip_rows = part(seq, 128, 128)
    c_kv = []
    for g in range(2):
        head = part(2 * c + g, 128, 128)
        c_kv.append((
            local(k_in.at[0, :, head], kb.at[g, chip_rows], 4 + 2 * g),
            local(v_in.at[0, :, head], vb.at[g, chip_rows], 5 + 2 * g),
        ))
    c_x = local(x_in.at[0], xv, 8)
    c_wd = local(wd_in, wd, 9)
    c_xc = local(
        x_in.at[0, :, part(x * 2 + c, 1024, 1024)], xcols.at[part(x * 2 + c, 128, 128)], 10
    )
    c_wq = local(wq_in.at[:, part(c, 2048, 2048)], wq, 11)
    c_wk = local(wk_in.at[:, part(c, 256, 256)], wk, 12)
    c_wv = local(wv_in.at[:, part(c, 256, 256)], wv, 13)

    barrier = pltpu.get_barrier_semaphore()
    peers = [sibling]
    for cc in range(2):
        peers += [at(x, (y + d) % NY, z, cc) for d in range(1, NY)]
        peers += [at((x + d) % NX, y, z, cc) for d in range(1, NX)]
        peers += [at(x, y, (z + d) % NZ, cc) for d in range(1, NZ)]
    for peer in peers:
        pl.semaphore_signal(
            barrier, inc=1, device_id=peer, device_id_type=pl.DeviceIdType.MESH
        )
    pl.semaphore_wait(barrier, len(peers))

    started = []

    def send(src, dst, ssem, rsem, device):
        copy = remote(src, dst, ssem, rsem, device)
        copy.start()
        started.append(copy)

    def kv_copy(g, which, yy, cc):
        source, target = ((k_in, kb), (v_in, vb))[which]
        return remote(
            source.at[0, :, part(2 * cc + g, 128, 128)],
            target.at[g, chip_rows],
            kv_s.at[g, which, yy * 2 + cc],
            kv_r.at[g, which, seq],
            at(x, yy, z, cc),
        )

    def each_later(body):
        for d in range(1, NY):
            @pl.when(y + d < NY)
            def _():
                body(y + d)

    for g in range(2):
        send(q_in.at[0, :, part(oc * 2 + g, 1024, 1024)],
             qb.at[my_rows, g * 1024:(g + 1) * 1024], sib_s.at[g], sib_r.at[g], sibling)
        send(g_in.at[0, :, part(oc * 2 + g, 1024, 1024)],
             gb.at[my_rows, g * 1024:(g + 1) * 1024], sib_s.at[2 + g], sib_r.at[2 + g], sibling)
        for which in range(2):
            copy = kv_copy(g, which, y, oc)
            copy.start()
            started.append(copy)

            def go(yy, g=g, which=which):
                for cc in range(2):
                    kv_copy(g, which, yy, cc).start()

            each_later(go)
        if g == 0:
            for d in range(NX):
                for cc in ([oc] if d == 0 else [0, 1]):
                    xx = (x + d) % NX
                    send(x_in.at[0, :, part(xx * 2 + cc, 1024, 1024)],
                         xcols.at[part(x * 2 + c, 128, 128)],
                         x_s.at[xx * 2 + cc], x_r.at[x * 2 + c], at(xx, y, z, cc))

    c_gown.wait()
    c_oown.wait()
    pick = (
        lax.broadcasted_iota(jnp.int32, (8, 1024), 1) // 128
        == lax.broadcasted_iota(jnp.int32, (8, 1024), 0)
    ).astype(BF)
    for chunk in range(4):
        cols = slice(chunk * 1024, (chunk + 1) * 1024)
        product = gown[:, cols].astype(F32) * oown[:, cols].astype(F32)
        high = product.astype(BF)
        low = (product - high.astype(F32)).astype(BF)
        deltas[chunk] = dot(pick, high, 1, 1) + dot(pick, low, 1, 1)
    for g in range(2):
        send(deltas.at[oc * 2 + g], deltas.at[4 + 2 * c + g], sib_s.at[4 + g], sib_r.at[4 + g], sibling)

    c_x.wait()
    c_wd.wait()
    total = jnp.zeros((128, 192), F32)
    for chunk in range(4):
        cols = slice(chunk * 2048, (chunk + 1) * 2048)
        total += dot(xv[:, cols], wd[cols, :], 1, 0)
    down_act[my_rows, :] = total.astype(BF)
    send(down_act.at[my_rows], down_act.at[my_rows], sib_s.at[6], sib_r.at[6], sibling)

    c_q.wait()
    c_g.wait()
    other_rows = part(oc, 128, 128)
    chip = part(y, 256, 256)

    def pair_of(ref, g, h):
        first = (g * 8 + h) * 128
        return jnp.concatenate(
            [ref[:, first:first + 128], ref[:, first + 128:first + 256]], axis=0
        )

    for g in range(2):
        arrived(qb.at[other_rows, g * 1024:(g + 1) * 1024], sib_r.at[g], sib_s.at[g])
        sib_rows = part(y * 2 + oc, 128, 128)
        c_kv[g][0].wait()
        arrived(kb.at[g, sib_rows], kv_r.at[g, 0, y * 2 + oc], kv_s.at[g, 0, 0])

        def scores_of(j, first, g=g):
            rows = part(j, 256, 256)
            keys = kb[g, rows, :]
            for h in range(0, 8, 2):
                qs = slice(h * 256, h * 256 + PAIR)
                s = dot(keys, pair_of(qb, g, h), 1, 1)
                if first:
                    key_at = lax.broadcasted_iota(jnp.int32, (256, PAIR), 0)
                    query_at = lax.broadcasted_iota(jnp.int32, (256, PAIR), 1) % 256
                    s = jnp.where(key_at <= query_at, s, -jnp.inf)
                scores[rows, qs] = s
                top = jnp.max(s, axis=0, keepdims=True)
                row_max[:, qs] = top if first else jnp.maximum(row_max[:, qs], top)

        scores_of(y, True)

        def more_scores(t, carry, g=g):
            j = y - 1 - t
            for cc in range(2):
                arrived(kb.at[g, part(j * 2 + cc, 128, 128)], kv_r.at[g, 0, j * 2 + cc], kv_s.at[g, 0, 0])
            scores_of(j, False)
            return carry

        lax.fori_loop(0, y, more_scores, 0)
        row_max[...] = row_max[...] * LOG2_SCALE

        def weights_of(j, sums):
            rows = part(j, 256, 256)
            found = []
            for h in range(0, 8, 2):
                qs = slice(h * 256, h * 256 + PAIR)
                w = jnp.exp2(scores[rows, qs] * LOG2_SCALE - row_max[:, qs])
                scores[rows, qs] = w
                found.append(jnp.sum(w, axis=0, keepdims=True))
            return sums + jnp.concatenate(found, axis=1)

        sums = lax.fori_loop(0, y + 1, weights_of, jnp.zeros((1, 2048), F32))
        row_max[...] = 1.0 / sums
        dq_acc[...] = jnp.zeros_like(dq_acc)

        arrived(gb.at[other_rows, g * 1024:(g + 1) * 1024], sib_r.at[2 + g], sib_s.at[2 + g])
        arrived(deltas.at[4 + 2 * oc + g], sib_r.at[4 + g], sib_s.at[4 + g])
        c_kv[g][1].wait()
        arrived(vb.at[g, sib_rows], kv_r.at[g, 1, y * 2 + oc], kv_s.at[g, 1, 0])
        mine = deltas[2 * c + g]
        theirs = deltas[4 + 2 * oc + g]
        low_half = jnp.where(c == 0, mine, theirs)
        high_half = jnp.where(c == 0, theirs, mine)
        delta_rows = [
            jnp.concatenate([low_half[h:h + 1], high_half[h:h + 1]], axis=1) for h in range(8)
        ]

        def grads_of(j, g=g, delta_rows=delta_rows):
            rows = part(j, 256, 256)
            keys, values = kb[g, rows, :], vb[g, rows, :]
            keys_t = keys.T
            value_sum = jnp.zeros((256, 128), F32)
            key_sum = jnp.zeros((256, 128), F32)
            for h in range(0, 8, 2):
                qs = slice(h * 256, h * 256 + PAIR)
                grad, query = pair_of(gb, g, h), pair_of(qb, g, h)
                prob_grad = dot(values, grad, 1, 1)
                prob = scores[rows, qs] * row_max[:, qs]
                delta = jnp.concatenate([delta_rows[h], delta_rows[h + 1]], axis=1)
                score_grad = (prob * (prob_grad - delta)).astype(BF)
                value_sum = value_sum + dot(prob.astype(BF), grad, 1, 0)
                key_sum = key_sum + dot(score_grad, query, 1, 0)
                dq_acc[:, qs] += dot(keys_t, score_grad, 1, 0)
            return key_sum * SCALE, value_sum

        def far_grads(j, carry, g=g):
            for cc in range(2):
                arrived(vb.at[g, part(j * 2 + cc, 128, 128)], kv_r.at[g, 1, j * 2 + cc], kv_s.at[g, 1, 0])
            key_sum, value_sum = grads_of(j)
            grads_out[g, j, 0] = key_sum.astype(BF)
            grads_out[g, j, 1] = value_sum.astype(BF)
            remote(grads_out.at[g, j], grads_in.at[g, y], gr_s.at[g, j], gr_r.at[g, y], at(x, j, z, c)).start()
            return carry

        lax.fori_loop(0, y, far_grads, 0)
        key_sum, value_sum = grads_of(y)
        own_grads[g, 0] = key_sum
        own_grads[g, 1] = value_sum
        for h in range(8):
            first = (g * 8 + h) * 128
            dq_rows[:, first:first + 128] = (
                dq_acc[:, h * 256:(h + 1) * 256].T * SCALE
            ).astype(BF)
        span = slice(g * 1024, (g + 1) * 1024)
        there = part(c * 2 + g, 1024, 1024)
        local(dq_rows.at[my_rows, span], dq_out.at[0, :, there], 14 + g)
        send(dq_rows.at[other_rows, span], dq_out.at[0, :, there], sib_s.at[7 + g], sib_r.at[7 + g], sibling)

    c_wq.wait()
    mid_part[:, 0:64] = dot(dq_rows[...], wq[...], 1, 1)
    arrived(down_act.at[other_rows], sib_r.at[6], sib_s.at[6])
    up_q = dot(down_act[:, 0:64], dq_rows[...], 0, 0).astype(BF)
    for k in range(NX):
        up_part[k, :, 0:2048] = up_q[k * 16:(k + 1) * 16, :]
        up_part[k, :, 2560:3072] = jnp.zeros((16, 512), BF)

    c_wk.wait()
    c_wv.wait()
    for g in range(2):
        def add_later(yy, g=g):
            arrived(grads_in.at[g, yy], gr_r.at[g, yy], gr_s.at[g, 0])
            for which in range(2):
                own_grads[g, which] = own_grads[g, which] + grads_in[g, yy, which].astype(F32)

        each_later(add_later)
        for which in range(2):
            kv_rows[which, :, g * 128:(g + 1) * 128] = own_grads[g, which].astype(BF)
    there = part(c, 256, 256)
    for which, out in ((0, dk_out), (1, dv_out)):
        local(kv_rows.at[which, my_rows], out.at[0, :, there], 16 + which)
        send(kv_rows.at[which, other_rows], out.at[0, :, there],
             sib_s.at[9 + which], sib_r.at[9 + which], sibling)
        weight = (wk, wv)[which]
        mid_part[:, 64 + 64 * which:128 + 64 * which] = dot(kv_rows[which], weight[...], 1, 1)
    send(mid_part, mid_sib, sib_s.at[11], sib_r.at[11], sibling)
    for which in range(2):
        up = dot(down_act[:, 64 + 64 * which:128 + 64 * which], kv_rows[which], 0, 0).astype(BF)
        for k in range(NX):
            up_part[k, :, 2048 + 256 * which:2304 + 256 * which] = up[k * 16:(k + 1) * 16, :]
    for d in range(1, NX):
        xx = (x + d) % NX
        send(up_part.at[xx], up_x.at[x], ux_s.at[xx], ux_r.at[x], at(xx, y, z, c))

    arrived(mid_sib, sib_r.at[11], sib_s.at[11])
    chip_tokens = part(x, 256, 256)
    mid_all[chip_tokens, :] = (mid_part[...] + mid_sib[...]).astype(BF)
    for d in range(1, NX):
        xx = (x + d) % NX
        send(mid_all.at[chip_tokens], mid_all.at[chip_tokens], mid_s.at[xx], mid_r.at[x], at(xx, y, z, c))

    up_x[x] = up_part[x]
    for d in range(1, NX):
        xx = (x + d) % NX
        arrived(up_x.at[xx], ux_r.at[xx], ux_s.at[0])
    summed = jnp.zeros((16, 3072), F32)
    for k in range(NX):
        summed = summed + up_x[k].astype(F32)
    summed = summed.astype(BF)
    for k in range(NZ):
        up_xsum[k] = summed[:, k * 384:(k + 1) * 384]
    for d in range(1, NZ):
        zz = (z + d) % NZ
        send(up_xsum.at[zz], up_z.at[z], uz_s.at[zz], uz_r.at[z], at(x, y, zz, c))

    c_xc.wait()
    for d in range(NX):
        xx = (x + d) % NX
        if d:
            arrived(mid_all.at[part(xx, 256, 256)], mid_r.at[xx], mid_s.at[0])
        for cc in ([oc] if d == 0 else [0, 1]):
            arrived(xcols.at[part(xx * 2 + cc, 128, 128)], x_r.at[xx * 2 + cc], x_s.at[0])
    mids = mid_all[...]
    for zz in range(4):
        found = dot(mids, xcols[:, zz * 256:(zz + 1) * 256], 0, 0).T
        for yy in range(NY):
            down_part[yy, zz] = found[yy * 64:(yy + 1) * 64, :].astype(BF)
    for d in range(1, NY):
        yy = (y + d) % NY
        send(down_part.at[yy], down_y.at[y], dy_s.at[yy], dy_r.at[y], at(x, yy, z, c))

    up_z[z] = up_xsum[z]
    for d in range(1, NZ):
        zz = (z + d) % NZ
        arrived(up_z.at[zz], uz_r.at[zz], uz_s.at[0])
    piece = jnp.zeros((16, 384), F32)
    for k in range(NZ):
        piece = piece + up_z[k].astype(F32)
    up_piece[...] = piece.astype(BF)
    up_y[y] = up_piece[...]
    for d in range(1, NY):
        yy = (y + d) % NY
        send(up_piece, up_y.at[y], uy_s.at[yy], uy_r.at[y], at(x, yy, z, c))

    down_y[y] = down_part[y]
    for d in range(1, NY):
        yy = (y + d) % NY
        arrived(down_y.at[yy], dy_r.at[yy], dy_s.at[0])
    part_sum = jnp.zeros((4, 64, 192), F32)
    for k in range(NY):
        part_sum = part_sum + down_y[k].astype(F32)
    down_z[...] = part_sum.astype(BF)
    for k in range(4):
        for cc in range(2):
            zz = 4 * c + k
            src = down_z.at[k, cc * 32:(cc + 1) * 32]

            @pl.when(jnp.logical_or(zz != z, cc != c))
            def _():
                remote(src, down_zin.at[z], dz_s.at[k, cc], dz_r.at[z], at(x, y, zz, cc)).start()

    for d in range(1, NY):
        yy = (y + d) % NY
        arrived(up_y.at[yy], uy_r.at[yy], uy_s.at[0])
    final = jnp.zeros((16, 384), F32)
    for k in range(NY):
        final = final + up_y[k].astype(F32)
    up_final[z] = (final * FACTOR).astype(BF)
    for d in range(1, NZ):
        zz = (z + d) % NZ
        send(up_final.at[z], up_final.at[z], az_s.at[zz], az_r.at[z], at(x, y, zz, c))

    source_core = z // 4

    @pl.when(source_core == c)
    def _():
        down_zin[z] = down_z[z % 4, part(c, 32, 32), :]

    for d in range(NZ):
        zz = (z + d) % NZ
        if d == 0:
            @pl.when(source_core != c)
            def _():
                arrived(down_zin.at[zz], dz_r.at[zz], dz_s.at[0, 0])
        else:
            arrived(down_zin.at[zz], dz_r.at[zz], dz_s.at[0, 0])
    down = jnp.zeros((32, 192), F32)
    for k in range(NZ):
        down = down + down_zin[k].astype(F32)
    down_out[...] = down * FACTOR

    for d in range(1, NZ):
        zz = (z + d) % NZ
        arrived(up_final.at[zz], az_r.at[zz], az_s.at[0])
    for k in range(NZ):
        up_slab[:, k * 384:(k + 1) * 384] = up_final[k]
    up_all[c, x] = up_slab[...]
    for d in range(1, NX):
        xx = (x + d) % NX
        send(up_slab, up_all.at[c, x], ax_s.at[xx], ax_r.at[x], at(xx, y, z, c))
    for d in range(1, NX):
        xx = (x + d) % NX
        arrived(up_all.at[c, xx], ax_r.at[xx], ax_s.at[0])
    send(up_all.at[c], up_all.at[c], sib_s.at[12], sib_r.at[12], sibling)
    arrived(up_all.at[oc], sib_r.at[12], sib_s.at[12])
    for cc in range(2):
        for k in range(NX):
            rows = slice(k * 16, (k + 1) * 16)
            upq_out[rows, cc * 2048:(cc + 1) * 2048] = up_all[cc, k, :, 0:2048].astype(F32)
            upk_out[rows, cc * 256:(cc + 1) * 256] = up_all[cc, k, :, 2048:2304].astype(F32)
            upv_out[rows, cc * 256:(cc + 1) * 256] = up_all[cc, k, :, 2304:2560].astype(F32)

    for copy in locals_[14:]:
        copy.wait()
    for g in range(2):
        there = part(oc * 2 + g, 1024, 1024)
        arrived(dq_out.at[0, :, there], sib_r.at[7 + g], sib_s.at[7 + g])
    there = part(oc, 256, 256)
    arrived(dk_out.at[0, :, there], sib_r.at[9], sib_s.at[9])
    arrived(dv_out.at[0, :, there], sib_r.at[10], sib_s.at[10])
    for copy in started:
        copy.wait_send()
    for g in range(2):
        for which in range(2):
            def sent(yy, g=g, which=which):
                for cc in range(2):
                    kv_copy(g, which, yy, cc).wait_send()

            each_later(sent)

        def grads_sent(j, carry, g=g):
            remote(grads_out.at[g, j], grads_in.at[g, y], gr_s.at[g, j], gr_r.at[g, y], at(x, j, z, c)).wait_send()
            return carry

        lax.fori_loop(0, y, grads_sent, 0)
    for k in range(4):
        for cc in range(2):
            zz = 4 * c + k
            src = down_z.at[k, cc * 32:(cc + 1) * 32]

            @pl.when(jnp.logical_or(zz != z, cc != c))
            def _():
                remote(src, down_zin.at[z], dz_s.at[k, cc], dz_r.at[z], at(x, y, zz, cc)).wait_send()


def body(x_in, q_in, k_in, v_in, o_in, g_in, wd, wq, wk, wv):
    vm = pltpu.VMEM
    dma = pltpu.SemaphoreType.DMA
    any_ = pl.BlockSpec(memory_space=pl.ANY)
    vmem = pl.BlockSpec(memory_space=pltpu.VMEM)
    shape = jax.ShapeDtypeStruct
    scratch = [
        vm((128, 8192), BF), vm((8192, 192), BF), vm((64, 2048), BF), vm((64, 256), BF),
        vm((64, 256), BF), vm((256, 2048), BF), vm((256, 2048), BF), vm((2, 1024, 128), BF),
        vm((2, 1024, 128), BF), vm((128, 4096), BF), vm((128, 4096), BF), vm((8, 8, 128), F32),
        vm((256, 192), BF),
        vm((1024, 1024), BF), vm((1024, 2048), F32), vm((1, 2048), F32), vm((128, 2048), F32),
        vm((256, 2048), BF), vm((2, 4, 2, 256, 128), BF), vm((2, 4, 2, 256, 128), BF),
        vm((2, 2, 256, 128), F32),
        vm((2, 256, 256), BF), vm((256, 192), F32), vm((256, 192), F32), vm((1024, 192), BF),
        vm((4, 4, 64, 192), BF), vm((4, 4, 64, 192), BF), vm((4, 64, 192), BF), vm((8, 32, 192), BF),
        vm((4, 16, 3072), BF), vm((4, 16, 3072), BF), vm((8, 16, 384), BF), vm((8, 16, 384), BF),
        vm((16, 384), BF), vm((4, 16, 384), BF), vm((8, 16, 384), BF), vm((16, 3072), BF),
        vm((2, 4, 16, 3072), BF),
        dma((18,)), dma((13,)), dma((13,)), dma((2, 2, 8)), dma((2, 2, 8)), dma((8,)), dma((8,)),
        dma((2, 4)), dma((2, 4)), dma((4,)), dma((4,)),
        dma((4,)), dma((4,)), dma((4, 2)), dma((8,)), dma((4,)), dma((4,)), dma((8,)), dma((8,)),
        dma((4,)), dma((4,)), dma((8,)), dma((8,)), dma((4,)), dma((4,)),
    ]
    return pl.pallas_call(
        kernel,
        out_shape=[
            shape((1, 128, 4096), BF), shape((1, 128, 512), BF), shape((1, 128, 512), BF),
            shape((32, 192), F32), shape((64, 4096), F32), shape((64, 512), F32),
            shape((64, 512), F32),
        ],
        in_specs=[any_] * 10,
        out_specs=[any_] * 3 + [vmem] * 4,
        scratch_shapes=scratch,
        compiler_params=pltpu.CompilerParams(
            vmem_limit_bytes=52 * 2**20, collective_id=0, has_side_effects=True
        ),
        cost_estimate=pl.CostEstimate(
            flops=8 * 10**9, bytes_accessed=12 * 2**20, transcendentals=4 * 2**20
        ),
    )(x_in, q_in, k_in, v_in, o_in, g_in, wd, wq, wk, wv)


def solution(mesh):
    token = P("dp", "seq", None)
    return jax.shard_map(
        body,
        mesh=mesh,
        in_specs=(token,) * 6 + (P(),) * 4,
        out_specs=(token,) * 3 + (P(("dp", "seq"), None), P(), P(), P()),
        check_vma=False,
    )
```

```python
import math

import jax
import jax.numpy as jnp
from jax import lax
from jax.experimental import pallas as pl
from jax.experimental.pallas import tpu as pltpu
from jax.sharding import PartitionSpec as P

BF = jnp.bfloat16
F32 = jnp.float32
HEAD = 128
SCALE = HEAD**-0.5
LOG2_SCALE = SCALE * math.log2(math.e)
FACTOR = 0.25 / math.sqrt(32768)
NX, NY, NZ = 4, 4, 8
ROWS = 2048


def dot(left, right, left_axis, right_axis):
    return lax.dot_general(
        left, right, (((left_axis,), (right_axis,)), ((), ())), preferred_element_type=F32
    )


def kernel(
    x_in, q_in, k_in, v_in, o_in, g_in, wd_in, wq_in, wk_in, wv_in,
    dq_out, dk_out, dv_out, down_out, up_out,
    xv, wd, wq, wk, wv, qb, gb, kb, vb, gown, oown, deltas, down_act,
    xcols, scores, row_max, delta_rows, dq_acc, dq_rows, grads_out, grads_in, own_grads,
    kv_rows, mid_part, mid_sib, mid_all, down_part, down_y, down_z, down_zin,
    up_part, up_y, up_sum, up_rs, up_fin,
    loc, sib_s, sib_r, kv_s, kv_r, x_s, x_r, gr_s, gr_r, mid_s, mid_r, fwd_s, fwd_r,
    dy_s, dy_r, dz_s, dz_r, uy_s, uy_r, us_s, us_r, ag_s, ag_r, ay_s, ay_r, sh_s, sh_r,
):
    dp = lax.axis_index("dp")
    seq = lax.axis_index("seq")
    x, z = dp // NZ, dp % NZ
    y, c = seq // 2, seq % 2
    oc = 1 - c

    def at(xx, yy, zz, cc):
        return {"dp": xx * NZ + zz, "seq": yy * 2 + cc}

    sibling = at(x, y, z, oc)

    def remote(src, dst, ssem, rsem, device):
        return pltpu.make_async_remote_copy(
            src_ref=src, dst_ref=dst, send_sem=ssem, recv_sem=rsem,
            device_id=device, device_id_type=pl.DeviceIdType.MESH,
        )

    def arrived(dst, rsem, ssem):
        remote(dst, dst, ssem, rsem, sibling).wait_recv()

    def part(start, size, unit):
        return pl.ds(pl.multiple_of(start * unit, unit), size)

    locals_ = []

    def local(src, dst, index):
        copy = pltpu.make_async_copy(src, dst, loc.at[index])
        copy.start()
        locals_.append(copy)
        return copy

    my_rows = part(c, 128, 128)
    c_gown = local(g_in.at[0], gown, 0)
    c_oown = local(o_in.at[0], oown, 1)
    c_q = local(q_in.at[0, :, part(c, 2048, 2048)], qb.at[my_rows], 2)
    c_g = local(g_in.at[0, :, part(c, 2048, 2048)], gb.at[my_rows], 3)
    chip_rows = part(seq, 128, 128)
    c_kv = []
    for g in range(2):
        head = part(2 * c + g, 128, 128)
        c_kv.append((
            local(k_in.at[0, :, head], kb.at[g, chip_rows], 4 + 2 * g),
            local(v_in.at[0, :, head], vb.at[g, chip_rows], 5 + 2 * g),
        ))
    c_x = local(x_in.at[0], xv, 8)
    c_wd = local(wd_in, wd, 9)
    c_xc = local(
        x_in.at[0, :, part(x * 2 + c, 1024, 1024)], xcols.at[part(x * 2 + c, 128, 128)], 10
    )
    c_wq = local(wq_in.at[:, part(c, 2048, 2048)], wq, 11)
    c_wk = local(wk_in.at[:, part(c, 256, 256)], wk, 12)
    c_wv = local(wv_in.at[:, part(c, 256, 256)], wv, 13)

    barrier = pltpu.get_barrier_semaphore()

    def greet(device):
        pl.semaphore_signal(
            barrier, inc=1, device_id=device, device_id_type=pl.DeviceIdType.MESH
        )

    greet(sibling)
    for d in range(1, NY):
        for cc in range(2):
            greet(at(x, (y + d) % NY, z, cc))
    for d in range(1, NX):
        greet(at((x + d) % NX, y, z, oc))
    for d in range(1, NZ):
        greet(at(x, y, (z + d) % NZ, oc))
    for d in range(1, NX * NZ):
        greet({"dp": (dp + d) % (NX * NZ), "seq": seq})
    pl.semaphore_wait(barrier, 1 + 2 * (NY - 1) + NX - 1 + NZ - 1 + NX * NZ - 1)

    started = []

    def send(src, dst, ssem, rsem, device):
        copy = remote(src, dst, ssem, rsem, device)
        copy.start()
        started.append(copy)

    def kv_copy(g, which, yy, cc):
        source, target = ((k_in, kb), (v_in, vb))[which]
        return remote(
            source.at[0, :, part(2 * cc + g, 128, 128)],
            target.at[g, chip_rows],
            kv_s.at[g, which, yy * 2 + cc],
            kv_r.at[g, which, seq],
            at(x, yy, z, cc),
        )

    def each_later(body):
        for d in range(1, NY):
            @pl.when(y + d < NY)
            def _():
                body(y + d)

    def send_kv(g, which):
        copy = kv_copy(g, which, y, oc)
        copy.start()
        started.append(copy)

        def go(yy):
            for cc in range(2):
                kv_copy(g, which, yy, cc).start()

        each_later(go)

    def span_of(g):
        return part(g, 1024, 1024)

    send_kv(0, 0)
    for g in range(2):
        send(q_in.at[0, :, span_of(oc * 2 + g)], qb.at[my_rows, span_of(g)],
             sib_s.at[g], sib_r.at[g], sibling)

    c_gown.wait()
    c_oown.wait()
    pick = (
        lax.broadcasted_iota(jnp.int32, (8, 1024), 1) // 128
        == lax.broadcasted_iota(jnp.int32, (8, 1024), 0)
    ).astype(BF)
    for chunk in range(4):
        if chunk == 2:
            send_kv(1, 0)
        cols = slice(chunk * 1024, (chunk + 1) * 1024)
        product = gown[:, cols].astype(F32) * oown[:, cols].astype(F32)
        high = product.astype(BF)
        low = (product - high.astype(F32)).astype(BF)
        deltas[chunk] = dot(pick, high, 1, 1) + dot(pick, low, 1, 1)
    for g in range(2):
        send(deltas.at[oc * 2 + g], deltas.at[4 + 2 * c + g], sib_s.at[4 + g], sib_r.at[4 + g], sibling)

    send_kv(0, 1)
    for g in range(2):
        send(g_in.at[0, :, span_of(oc * 2 + g)], gb.at[my_rows, span_of(g)],
             sib_s.at[2 + g], sib_r.at[2 + g], sibling)
    c_x.wait()
    c_wd.wait()
    total = jnp.zeros((128, 192), F32)
    for chunk in range(4):
        cols = slice(chunk * 2048, (chunk + 1) * 2048)
        total += dot(xv[:, cols], wd[:, cols], 1, 1)
    down_act[my_rows, :] = total.astype(BF)
    send(down_act.at[my_rows], down_act.at[my_rows], sib_s.at[6], sib_r.at[6], sibling)
    send_kv(1, 1)
    for d in range(NX):
        for cc in ([oc] if d == 0 else [0, 1]):
            xx = (x + d) % NX
            send(x_in.at[0, :, part(xx * 2 + cc, 1024, 1024)],
                 xcols.at[part(x * 2 + c, 128, 128)],
                 x_s.at[xx * 2 + cc], x_r.at[x * 2 + c], at(xx, y, z, cc))

    c_q.wait()
    c_g.wait()
    other_rows = part(oc, 128, 128)

    def heads_of(ref, g):
        return jnp.concatenate(
            [ref[:, part(g * 8 + h, 128, 128)] for h in range(8)], axis=0
        )

    sib_rows = part(y * 2 + oc, 128, 128)
    for g in range(2):
        c_kv[g][0].wait()
        c_kv[g][1].wait()

    def scores_of(g, j, first):
        rows = part(j, 256, 256)
        s = dot(kb[g, rows, :], heads_of(qb, g), 1, 1)
        if first:
            key_at = lax.broadcasted_iota(jnp.int32, (256, ROWS), 0)
            query_at = lax.broadcasted_iota(jnp.int32, (256, ROWS), 1) % 256
            s = jnp.where(key_at <= query_at, s, -jnp.inf)
        scores[g, rows, :] = s
        top = jnp.max(s, axis=0, keepdims=True)
        row_max[g] = top if first else jnp.maximum(row_max[g], top)

    def own_scores(g, carry):
        arrived(qb.at[other_rows, span_of(g)], sib_r.at[g], sib_s.at[g])
        arrived(kb.at[g, sib_rows], kv_r.at[g, 0, y * 2 + oc], kv_s.at[g, 0, 0])
        scores_of(g, y, True)
        return carry

    lax.fori_loop(0, 2, own_scores, 0)

    def all_weights(g, carry):
        def more_scores(t, inner):
            j = y - 1 - t
            for cc in range(2):
                arrived(kb.at[g, part(j * 2 + cc, 128, 128)], kv_r.at[g, 0, j * 2 + cc], kv_s.at[g, 0, 0])
            scores_of(g, j, False)
            return inner

        lax.fori_loop(0, y, more_scores, 0)
        row_max[g] = row_max[g] * LOG2_SCALE

        def weights_of(j, sums):
            rows = part(j, 256, 256)
            found = []
            for h in range(0, 8, 2):
                qs = slice(h * 256, h * 256 + 512)
                w = jnp.exp2(scores[g, rows, qs] * LOG2_SCALE - row_max[g, :, qs])
                scores[g, rows, qs] = w
                found.append(jnp.sum(w, axis=0, keepdims=True))
            return sums + jnp.concatenate(found, axis=1)

        sums = lax.fori_loop(0, y + 1, weights_of, jnp.zeros((1, 2048), F32))
        row_max[g] = 1.0 / sums
        dq_acc[g] = jnp.zeros((128, 2048), F32)
        return carry

    lax.fori_loop(0, 2, all_weights, 0)

    def grads_of(g, j):
        rows = part(j, 256, 256)
        keys, values = kb[g, rows, :], vb[g, rows, :]
        grad, query = heads_of(gb, g), heads_of(qb, g)
        prob_grad = dot(values, grad, 1, 1)
        prob = scores[g, rows, :] * row_max[g]
        score_grad = (prob * (prob_grad - delta_rows[g])).astype(BF)
        value_sum = dot(prob.astype(BF), grad, 1, 0)
        key_sum = dot(score_grad, query, 1, 0)
        dq_acc[g] = dq_acc[g] + dot(keys.T, score_grad, 1, 0)
        return key_sum * SCALE, value_sum

    def grads_copy(g, j):
        return remote(
            grads_out.at[g, j], grads_in.at[g, y], gr_s.at[g, j], gr_r.at[g, y], at(x, j, z, c)
        )

    def other_grads(g, carry):
        arrived(gb.at[other_rows, span_of(g)], sib_r.at[2 + g], sib_s.at[2 + g])
        arrived(deltas.at[4 + 2 * oc + g], sib_r.at[4 + g], sib_s.at[4 + g])
        arrived(vb.at[g, sib_rows], kv_r.at[g, 1, y * 2 + oc], kv_s.at[g, 1, 0])
        mine = deltas[2 * c + g]
        theirs = deltas[4 + 2 * oc + g]
        low_half = jnp.where(c == 0, mine, theirs)
        high_half = jnp.where(c == 0, theirs, mine)
        for h in range(8):
            delta_rows[g, :, h * 256:h * 256 + 128] = low_half[h:h + 1]
            delta_rows[g, :, h * 256 + 128:(h + 1) * 256] = high_half[h:h + 1]

        def far_grads(j, inner):
            for cc in range(2):
                arrived(vb.at[g, part(j * 2 + cc, 128, 128)], kv_r.at[g, 1, j * 2 + cc], kv_s.at[g, 1, 0])
            key_sum, value_sum = grads_of(g, j)
            grads_out[g, j, 0] = key_sum.astype(BF)
            grads_out[g, j, 1] = value_sum.astype(BF)
            grads_copy(g, j).start()
            return inner

        lax.fori_loop(0, y, far_grads, 0)
        return carry

    lax.fori_loop(0, 2, other_grads, 0)

    def last_grads(g, carry):
        key_sum, value_sum = grads_of(g, y)
        own_grads[g, 0] = key_sum
        own_grads[g, 1] = value_sum
        return carry

    lax.fori_loop(0, 2, last_grads, 0)
    for g in range(2):
        for h in range(8):
            first = (g * 8 + h) * 128
            dq_rows[:, first:first + 128] = (
                dq_acc[g, :, h * 256:(h + 1) * 256].T * SCALE
            ).astype(BF)

    arrived(down_act.at[other_rows], sib_r.at[6], sib_s.at[6])

    def put_tiles(term, first):
        for k in range(NY):
            for t in range(term.shape[1] // 128):
                up_part[k, first + t] = term[k * 16:(k + 1) * 16, t * 128:(t + 1) * 128]

    def send_group(e):
        tiles = pl.ds(e * 5, 5)
        for d in range(1, NY):
            yy = (y + d) % NY
            send(up_part.at[yy, tiles], up_y.at[y, tiles], uy_s.at[yy, e], uy_r.at[y, e],
                 at(x, yy, z, c))

    put_tiles(dot(down_act[:, 0:64], dq_rows[...], 0, 0).astype(BF), 0)
    for e in range(3):
        send_group(e)
    c_wq.wait()
    mid_part[:, 0:64] = dot(dq_rows[...], wq[...], 1, 1)

    c_wk.wait()
    c_wv.wait()
    for g in range(2):
        def add_later(yy, g=g):
            arrived(grads_in.at[g, yy], gr_r.at[g, yy], gr_s.at[g, 0])
            for which in range(2):
                own_grads[g, which] = own_grads[g, which] + grads_in[g, yy, which].astype(F32)

        each_later(add_later)
        for which in range(2):
            kv_rows[which, :, g * 128:(g + 1) * 128] = own_grads[g, which].astype(BF)
    for which in range(2):
        weight = (wk, wv)[which]
        mid_part[:, 64 + 64 * which:128 + 64 * which] = dot(kv_rows[which], weight[...], 1, 1)
    send(mid_part, mid_sib, sib_s.at[11], sib_r.at[11], sibling)
    for which in range(2):
        act = down_act[:, 64 + 64 * which:128 + 64 * which]
        put_tiles(dot(act, kv_rows[which], 0, 0).astype(BF), 16 + 2 * which)
    send_group(3)

    arrived(mid_sib, sib_r.at[11], sib_s.at[11])
    mid_all[part(x, 256, 256), :] = (mid_part[...] + mid_sib[...]).astype(BF)
    mid_rows = part(x * 2 + c, 128, 128)
    for d in range(1, NX):
        xx = (x + d) % NX
        send(mid_all.at[mid_rows], mid_all.at[mid_rows], mid_s.at[xx], mid_r.at[x], at(xx, y, z, c))

    for g in range(2):
        span = slice(g * 1024, (g + 1) * 1024)
        there = part(c * 2 + g, 1024, 1024)
        local(dq_rows.at[my_rows, span], dq_out.at[0, :, there], 14 + g)
        send(dq_rows.at[other_rows, span], dq_out.at[0, :, there], sib_s.at[7 + g], sib_r.at[7 + g], sibling)
    there = part(c, 256, 256)
    for which, out in ((0, dk_out), (1, dv_out)):
        local(kv_rows.at[which, my_rows], out.at[0, :, there], 16 + which)
        send(kv_rows.at[which, other_rows], out.at[0, :, there],
             sib_s.at[9 + which], sib_r.at[9 + which], sibling)

    def owner_of(k):
        return (k // 5) * NZ + k % 5

    def to_owner(k):
        return remote(
            up_sum.at[k], up_rs.at[dp], us_s.at[k], us_r.at[dp], {"dp": owner_of(k), "seq": seq}
        )

    def send_tile(k, carry):
        @pl.when(owner_of(k) != dp)
        def _():
            to_owner(k).start()
        return carry

    for e in range(4):
        tiles = pl.ds(e * 5, 5)
        up_y[y, tiles] = up_part[y, tiles]
        for d in range(1, NY):
            yy = (y + d) % NY
            arrived(up_y.at[yy, tiles], uy_r.at[yy, e], uy_s.at[0, 0])
        first, second = up_y[0, tiles].astype(F32), up_y[1, tiles].astype(F32)
        third, fourth = up_y[2, tiles].astype(F32), up_y[3, tiles].astype(F32)
        up_sum[tiles] = ((first + second) + (third + fourth)).astype(BF)
        lax.fori_loop(e * 5, e * 5 + 5, send_tile, 0)

    c_xc.wait()
    for d in range(1, NX):
        xx = (x + d) % NX
        rows = part(xx * 2 + c, 128, 128)
        arrived(mid_all.at[rows], mid_r.at[xx], mid_s.at[0])
        send(mid_all.at[rows], mid_all.at[rows], fwd_s.at[xx], fwd_r.at[xx], sibling)
    for d in range(NX):
        xx = (x + d) % NX
        for cc in ([oc] if d == 0 else [0, 1]):
            arrived(xcols.at[part(xx * 2 + cc, 128, 128)], x_r.at[xx * 2 + cc], x_s.at[0])
    for d in range(1, NX):
        xx = (x + d) % NX
        arrived(mid_all.at[part(xx * 2 + oc, 128, 128)], fwd_r.at[xx], fwd_s.at[0])
    mids = mid_all[...]
    for zz in range(4):
        found = dot(mids, xcols[:, zz * 256:(zz + 1) * 256], 0, 0).T
        for yy in range(NY):
            down_part[yy, zz] = found[yy * 64:(yy + 1) * 64, :].astype(BF)
        for d in range(1, NY):
            yy = (y + d) % NY
            send(down_part.at[yy, zz], down_y.at[y, zz], dy_s.at[yy, zz], dy_r.at[y, zz],
                 at(x, yy, z, c))

    own_tile = x * 5 + z
    owns = z < 5

    def final_copy(d):
        other = (dp + d) % (NX * NZ)
        return remote(
            up_fin.at[own_tile], up_fin.at[own_tile], ag_s.at[other], ag_r.at[own_tile],
            {"dp": other, "seq": seq},
        )

    @pl.when(owns)
    def _():
        up_rs[dp] = up_sum[own_tile]

        def wait_one(d, carry):
            other = (dp + d) % (NX * NZ)
            arrived(up_rs.at[other], us_r.at[other], us_s.at[0])
            return carry

        lax.fori_loop(1, NX * NZ, wait_one, 0)
        tile = jnp.sum(up_rs[...].astype(F32), axis=0)
        up_fin[own_tile] = (tile * FACTOR).astype(BF)

        def send_one(d, carry):
            final_copy(d).start()
            return carry

        lax.fori_loop(1, NX * NZ, send_one, 0)

    def down_copy(k, cc):
        return remote(
            down_z.at[k, cc * 32:(cc + 1) * 32], down_zin.at[z], dz_s.at[k, cc], dz_r.at[z],
            at(x, y, 4 * c + k, cc),
        )

    def wait_tile(k, carry):
        @pl.when(owner_of(k) != dp)
        def _():
            arrived(up_fin.at[k], ag_r.at[k], ag_s.at[0])
        return carry

    for k in range(4):
        down_y[y, k] = down_part[y, k]
        for d in range(1, NY):
            yy = (y + d) % NY
            arrived(down_y.at[yy, k], dy_r.at[yy, k], dy_s.at[0, 0])
        first, second = down_y[0, k].astype(F32), down_y[1, k].astype(F32)
        third, fourth = down_y[2, k].astype(F32), down_y[3, k].astype(F32)
        down_z[k] = ((first + second) + (third + fourth)).astype(BF)
        for cc in range(2):
            @pl.when(jnp.logical_or(4 * c + k != z, cc != c))
            def _():
                down_copy(k, cc).start()

        tiles = pl.ds(k * 5, 5)
        lax.fori_loop(k * 5, k * 5 + 5, wait_tile, 0)
        for d in range(1, NY):
            yy = (y + d) % NY
            send(up_fin.at[tiles], up_out.at[c, y, tiles], ay_s.at[yy, k], ay_r.at[y, k],
                 at(x, yy, z, c))
        local(up_fin.at[tiles], up_out.at[c, y, tiles], 18 + k)
        send(up_fin.at[tiles], up_out.at[c, y, tiles], sh_s.at[y, k], sh_r.at[y, k], sibling)

    source_core = z // 4

    @pl.when(source_core == c)
    def _():
        down_zin[z] = down_z[z % 4, part(c, 32, 32), :]

    for d in range(NZ):
        zz = (z + d) % NZ
        if d == 0:
            @pl.when(source_core != c)
            def _():
                arrived(down_zin.at[zz], dz_r.at[zz], dz_s.at[0, 0])
        else:
            arrived(down_zin.at[zz], dz_r.at[zz], dz_s.at[0, 0])
    down_out[...] = jnp.sum(down_zin[...].astype(F32), axis=0) * FACTOR

    for e in range(4):
        tiles = pl.ds(e * 5, 5)
        for d in range(1, NY):
            yy = (y + d) % NY
            arrived(up_out.at[c, yy, tiles], ay_r.at[yy, e], ay_s.at[0, 0])
            send(up_out.at[c, yy, tiles], up_out.at[c, yy, tiles], sh_s.at[yy, e], sh_r.at[yy, e],
                 sibling)

    for copy in locals_[14:]:
        copy.wait()
    for g in range(2):
        there = part(oc * 2 + g, 1024, 1024)
        arrived(dq_out.at[0, :, there], sib_r.at[7 + g], sib_s.at[7 + g])
    there = part(oc, 256, 256)
    arrived(dk_out.at[0, :, there], sib_r.at[9], sib_s.at[9])
    arrived(dv_out.at[0, :, there], sib_r.at[10], sib_s.at[10])
    for copy in started:
        copy.wait_send()
    for g in range(2):
        for which in range(2):
            def sent(yy, g=g, which=which):
                for cc in range(2):
                    kv_copy(g, which, yy, cc).wait_send()

            each_later(sent)

        def grads_sent(j, carry, g=g):
            grads_copy(g, j).wait_send()
            return carry

        lax.fori_loop(0, y, grads_sent, 0)

    def tile_sent(k, carry):
        @pl.when(owner_of(k) != dp)
        def _():
            to_owner(k).wait_send()
        return carry

    lax.fori_loop(0, 20, tile_sent, 0)

    @pl.when(owns)
    def _():
        def final_sent(d, carry):
            final_copy(d).wait_send()
            return carry

        lax.fori_loop(1, NX * NZ, final_sent, 0)

    for k in range(4):
        for cc in range(2):
            @pl.when(jnp.logical_or(4 * c + k != z, cc != c))
            def _():
                down_copy(k, cc).wait_send()
    for d in range(NY):
        yy = (y + d) % NY
        for e in range(4):
            arrived(up_out.at[oc, yy, pl.ds(e * 5, 5)], sh_r.at[yy, e], sh_s.at[0, 0])


def finish(
    dq_in, dk_in, dv_in, down_in, up_in, dq, dk, dv, down, upq, upk, upv,
    dq_v, dk_v, dv_v, up_v, upq_v, upk_v, upv_v, in_s, out_s,
):
    ins = [pltpu.make_async_copy(up_in, up_v, in_s.at[0])]
    outs = []
    for k in range(4):
        cols = pl.ds(k * 1024, 1024)
        ins.append(
            pltpu.make_async_copy(dq_in.at[:, :, cols], dq_v.at[:, :, cols], in_s.at[1 + k])
        )
        outs.append(pltpu.make_async_copy(dq_v.at[:, :, cols], dq.at[:, :, cols], out_s.at[k]))
    for k, (src, mid, dst) in enumerate(((dk_in, dk_v, dk), (dv_in, dv_v, dv))):
        ins.append(pltpu.make_async_copy(src, mid, in_s.at[5 + k]))
        outs.append(pltpu.make_async_copy(mid, dst, out_s.at[4 + k]))
    ups = [
        pltpu.make_async_copy(
            upq_v.at[pl.ds(k * 16, 16)], upq.at[pl.ds(k * 16, 16)], out_s.at[6 + k]
        )
        for k in range(NY)
    ]
    ups += [
        pltpu.make_async_copy(upk_v, upk, out_s.at[10]),
        pltpu.make_async_copy(upv_v, upv, out_s.at[11]),
    ]
    for copy in ins:
        copy.start()
    down[...] = down_in[...]
    for arriving, leaving in zip(ins[1:], outs):
        arriving.wait()
        leaving.start()
    ins[0].wait()
    for k in range(NY):
        rows = slice(k * 16, (k + 1) * 16)
        for cc in range(2):
            for t in range(20):
                tile = up_v[cc, k, t].astype(F32)
                if t < 16:
                    upq_v[rows, cc * 2048 + t * 128:cc * 2048 + (t + 1) * 128] = tile
                else:
                    first = cc * 256 + (t % 2) * 128
                    (upk_v if t < 18 else upv_v)[rows, first:first + 128] = tile
        ups[k].start()
    for copy in ups[4:]:
        copy.start()
    for copy in outs + ups:
        copy.wait()


def body(x_in, q_in, k_in, v_in, o_in, g_in, wd, wq, wk, wv):
    vm = pltpu.VMEM
    dma = pltpu.SemaphoreType.DMA
    any_ = pl.BlockSpec(memory_space=pl.ANY)
    vmem = pl.BlockSpec(memory_space=pltpu.VMEM)
    shape = jax.ShapeDtypeStruct
    scratch = [
        vm((128, 8192), BF), vm((192, 8192), BF), vm((64, 2048), BF), vm((64, 256), BF),
        vm((64, 256), BF), vm((256, 2048), BF), vm((256, 2048), BF), vm((2, 1024, 128), BF),
        vm((2, 1024, 128), BF), vm((128, 4096), BF), vm((128, 4096), BF), vm((8, 8, 128), F32),
        vm((256, 192), BF),
        vm((1024, 1024), BF), vm((2, 1024, 2048), F32), vm((2, 1, 2048), F32),
        vm((2, 1, 2048), F32),
        vm((2, 128, 2048), F32),
        vm((256, 2048), BF), vm((2, 4, 2, 256, 128), BF), vm((2, 4, 2, 256, 128), BF),
        vm((2, 2, 256, 128), F32),
        vm((2, 256, 256), BF), vm((256, 192), F32), vm((256, 192), F32), vm((1024, 192), BF),
        vm((4, 4, 64, 192), BF), vm((4, 4, 64, 192), BF), vm((4, 64, 192), BF), vm((8, 32, 192), BF),
        vm((4, 20, 16, 128), BF), vm((4, 20, 16, 128), BF), vm((20, 16, 128), BF),
        vm((32, 16, 128), BF), vm((20, 16, 128), BF),
        dma((22,)), dma((12,)), dma((12,)), dma((2, 2, 8)), dma((2, 2, 8)), dma((8,)), dma((8,)),
        dma((2, 4)), dma((2, 4)), dma((4,)), dma((4,)), dma((4,)), dma((4,)),
        dma((4, 4)), dma((4, 4)), dma((4, 2)), dma((8,)), dma((4, 4)), dma((4, 4)), dma((20,)), dma((32,)),
        dma((32,)), dma((20,)), dma((4, 4)), dma((4, 4)), dma((4, 4)), dma((4, 4)),
    ]
    first = pl.pallas_call(
        kernel,
        out_shape=[
            shape((1, 128, 4096), BF), shape((1, 128, 512), BF), shape((1, 128, 512), BF),
            shape((32, 192), F32), shape((2, 4, 20, 16, 128), BF),
        ],
        in_specs=[any_] * 10,
        out_specs=[any_] * 3 + [vmem, any_],
        scratch_shapes=scratch,
        compiler_params=pltpu.CompilerParams(
            vmem_limit_bytes=60 * 2**20, collective_id=0, has_side_effects=True
        ),
        cost_estimate=pl.CostEstimate(
            flops=8 * 10**9, bytes_accessed=12 * 2**20, transcendentals=4 * 2**20
        ),
    )(x_in, q_in, k_in, v_in, o_in, g_in, wd.T, wq, wk, wv)
    return pl.pallas_call(
        finish,
        out_shape=[
            shape((1, 128, 4096), BF), shape((1, 128, 512), BF), shape((1, 128, 512), BF),
            shape((32, 192), F32), shape((64, 4096), F32), shape((64, 512), F32),
            shape((64, 512), F32),
        ],
        in_specs=[any_] * 3 + [vmem, any_],
        out_specs=[any_] * 3 + [vmem] + [any_] * 3,
        scratch_shapes=[
            vm((1, 128, 4096), BF), vm((1, 128, 512), BF), vm((1, 128, 512), BF),
            vm((2, 4, 20, 16, 128), BF), vm((64, 4096), F32), vm((64, 512), F32),
            vm((64, 512), F32), dma((7,)), dma((12,)),
        ],
        compiler_params=pltpu.CompilerParams(vmem_limit_bytes=60 * 2**20),
        cost_estimate=pl.CostEstimate(flops=10**6, bytes_accessed=6 * 2**20, transcendentals=0),
    )(*first)


def solution(mesh):
    token = P("dp", "seq", None)
    return jax.shard_map(
        body,
        mesh=mesh,
        in_specs=(token,) * 6 + (P(),) * 4,
        out_specs=(token,) * 3 + (P(("dp", "seq"), None), P(), P(), P()),
        check_vma=False,
    )
```

```python
import math

import jax
import jax.numpy as jnp
from jax import lax
from jax.experimental import pallas as pl
from jax.experimental.pallas import tpu as pltpu
from jax.sharding import PartitionSpec as P

BF = jnp.bfloat16
F32 = jnp.float32
HEAD = 128
SCALE = HEAD**-0.5
LOG2_SCALE = SCALE * math.log2(math.e)
FACTOR = 0.25 / math.sqrt(32768)
NX, NY, NZ = 4, 4, 8
ROWS = 2048


def dot(left, right, left_axis, right_axis):
    return lax.dot_general(
        left, right, (((left_axis,), (right_axis,)), ((), ())), preferred_element_type=F32
    )


def kernel(
    x_in, q_in, k_in, v_in, o_in, g_in, wd_in, wq_in, wk_in, wv_in,
    dq_out, dk_out, dv_out, down_out, up_out,
    xv, wd, wq, wk, wv, qb, gb, kb, vb, gown, oown, deltas, down_act,
    xcols, scores, row_max, delta_rows, dq_acc, dq_rows, grads_out, grads_in, own_grads,
    kv_rows, mid_part, mid_sib, mid_all, down_part, down_y, down_z, down_zin,
    up_part, up_y, up_sum, up_rs, up_fin,
    loc, sib_s, sib_r, kv_s, kv_r, x_s, x_r, gr_s, gr_r, mid_s, mid_r, fwd_s, fwd_r,
    dy_s, dy_r, dz_s, dz_r, uy_s, uy_r, us_s, us_r, ag_s, ag_r, ay_s, ay_r, sh_s, sh_r,
):
    dp = lax.axis_index("dp")
    seq = lax.axis_index("seq")
    x, z = dp // NZ, dp % NZ
    y, c = seq // 2, seq % 2
    oc = 1 - c

    def at(xx, yy, zz, cc):
        return {"dp": xx * NZ + zz, "seq": yy * 2 + cc}

    sibling = at(x, y, z, oc)

    def remote(src, dst, ssem, rsem, device):
        return pltpu.make_async_remote_copy(
            src_ref=src, dst_ref=dst, send_sem=ssem, recv_sem=rsem,
            device_id=device, device_id_type=pl.DeviceIdType.MESH,
        )

    def arrived(dst, rsem):
        remote(dst, dst, sib_s.at[0], rsem, sibling).wait_recv()

    def left(src, ssem):
        remote(src, src, ssem, sib_r.at[0], sibling).wait_send()

    def part(start, size, unit):
        return pl.ds(pl.multiple_of(start * unit, unit), size)

    locals_ = []

    def local(src, dst, index):
        copy = pltpu.make_async_copy(src, dst, loc.at[index])
        copy.start()
        locals_.append(copy)
        return copy

    my_rows = part(c, 128, 128)
    c_gown = local(g_in.at[0], gown, 0)
    c_oown = local(o_in.at[0], oown, 1)
    c_q = local(q_in.at[0, :, part(c, 2048, 2048)], qb.at[my_rows], 2)
    c_g = local(g_in.at[0, :, part(c, 2048, 2048)], gb.at[my_rows], 3)
    chip_rows = part(seq, 128, 128)
    c_kv = []
    for g in range(2):
        head = part(2 * c + g, 128, 128)
        c_kv.append((
            local(k_in.at[0, :, head], kb.at[g, chip_rows], 4 + 2 * g),
            local(v_in.at[0, :, head], vb.at[g, chip_rows], 5 + 2 * g),
        ))
    c_x = local(x_in.at[0], xv, 8)
    c_wd = local(wd_in, wd, 9)
    c_xc = local(
        x_in.at[0, :, part(x * 2 + c, 1024, 1024)], xcols.at[part(x * 2 + c, 128, 128)], 10
    )
    c_wq = local(wq_in.at[:, part(c, 2048, 2048)], wq, 11)
    c_wk = local(wk_in.at[:, part(c, 256, 256)], wk, 12)
    c_wv = local(wv_in.at[:, part(c, 256, 256)], wv, 13)

    barrier = pltpu.get_barrier_semaphore()

    def greet(device):
        pl.semaphore_signal(
            barrier, inc=1, device_id=device, device_id_type=pl.DeviceIdType.MESH
        )

    greet(sibling)
    for d in range(1, NY):
        for cc in range(2):
            greet(at(x, (y + d) % NY, z, cc))
    for d in range(1, NX):
        greet(at((x + d) % NX, y, z, oc))
    for d in range(1, NZ):
        greet(at(x, y, (z + d) % NZ, oc))
    for d in range(1, NX * NZ):
        greet({"dp": (dp + d) % (NX * NZ), "seq": seq})
    pl.semaphore_wait(barrier, 1 + 2 * (NY - 1) + NX - 1 + NZ - 1 + NX * NZ - 1)

    started = []

    def send(src, dst, ssem, rsem, device, alone=False):
        copy = remote(src, dst, ssem, rsem, device)
        copy.start()
        if alone:
            started.append(copy)

    def kv_copy(g, which, yy, cc):
        source, target = ((k_in, kb), (v_in, vb))[which]
        return remote(
            source.at[0, :, part(2 * cc + g, 128, 128)],
            target.at[g, chip_rows],
            kv_s.at[yy],
            kv_r.at[g, which, y],
            at(x, yy, z, cc),
        )

    def each_later(body):
        for d in range(1, NY):
            @pl.when(y + d < NY)
            def _():
                body(y + d)

    def send_kv(g, which):
        kv_copy(g, which, y, oc).start()

        def go(yy):
            for cc in range(2):
                kv_copy(g, which, yy, cc).start()

        each_later(go)

    def span_of(g):
        return part(g, 1024, 1024)

    for g in range(2):
        send(q_in.at[0, :, span_of(oc * 2 + g)], qb.at[my_rows, span_of(g)],
             sib_s.at[g], sib_r.at[g], sibling, True)
        for which in range(2):
            send_kv(g, which)
        send(g_in.at[0, :, span_of(oc * 2 + g)], gb.at[my_rows, span_of(g)],
             sib_s.at[2 + g], sib_r.at[2 + g], sibling, True)

    c_gown.wait()
    c_oown.wait()
    pick = (
        lax.broadcasted_iota(jnp.int32, (8, 1024), 1) // 128
        == lax.broadcasted_iota(jnp.int32, (8, 1024), 0)
    ).astype(BF)
    for chunk in range(4):
        cols = slice(chunk * 1024, (chunk + 1) * 1024)
        product = gown[:, cols].astype(F32) * oown[:, cols].astype(F32)
        high = product.astype(BF)
        low = (product - high.astype(F32)).astype(BF)
        deltas[chunk] = dot(pick, high, 1, 1) + dot(pick, low, 1, 1)
    for g in range(2):
        send(deltas.at[oc * 2 + g], deltas.at[4 + 2 * c + g], sib_s.at[4 + g], sib_r.at[4 + g], sibling, True)

    c_x.wait()
    c_wd.wait()
    total = jnp.zeros((128, 192), F32)
    for chunk in range(4):
        cols = slice(chunk * 2048, (chunk + 1) * 2048)
        total += dot(xv[:, cols], wd[:, cols], 1, 1)
    down_act[my_rows, :] = total.astype(BF)
    send(down_act.at[my_rows], down_act.at[my_rows], sib_s.at[6], sib_r.at[6], sibling, True)
    for d in range(NX):
        for cc in ([oc] if d == 0 else [0, 1]):
            xx = (x + d) % NX
            send(x_in.at[0, :, part(xx * 2 + cc, 1024, 1024)],
                 xcols.at[part(x * 2 + c, 128, 128)],
                 x_s.at[0], x_r.at[0], at(xx, y, z, cc))

    c_q.wait()
    c_g.wait()
    other_rows = part(oc, 128, 128)

    def heads_of(ref, g):
        return jnp.concatenate(
            [ref[:, part(g * 8 + h, 128, 128)] for h in range(8)], axis=0
        )

    sib_rows = part(y * 2 + oc, 128, 128)
    for g in range(2):
        c_kv[g][0].wait()
        c_kv[g][1].wait()

    def scores_of(g, j, first):
        rows = part(j, 256, 256)
        s = dot(kb[g, rows, :], heads_of(qb, g), 1, 1)
        if first:
            key_at = lax.broadcasted_iota(jnp.int32, (256, ROWS), 0)
            query_at = lax.broadcasted_iota(jnp.int32, (256, ROWS), 1) % 256
            s = jnp.where(key_at <= query_at, s, -jnp.inf)
        scores[g, rows, :] = s
        top = jnp.max(s, axis=0, keepdims=True)
        row_max[g] = top if first else jnp.maximum(row_max[g], top)

    def own_scores(g, carry):
        arrived(qb.at[other_rows, span_of(g)], sib_r.at[g])
        arrived(kb.at[g, sib_rows], kv_r.at[g, 0, y])
        scores_of(g, y, True)
        return carry

    lax.fori_loop(0, 2, own_scores, 0)

    def all_weights(g):
        def more_scores(t, inner):
            j = y - 1 - t
            arrived(kb.at[g, part(j, 256, 256)], kv_r.at[g, 0, j])
            scores_of(g, j, False)
            return inner

        lax.fori_loop(0, y, more_scores, 0)
        row_max[g] = row_max[g] * LOG2_SCALE

        def weights_of(j, sums):
            rows = part(j, 256, 256)
            found = []
            for h in range(0, 8, 2):
                qs = slice(h * 256, h * 256 + 512)
                w = jnp.exp2(scores[g, rows, qs] * LOG2_SCALE - row_max[g, :, qs])
                scores[g, rows, qs] = w
                found.append(jnp.sum(w, axis=0, keepdims=True))
            return sums + jnp.concatenate(found, axis=1)

        sums = lax.fori_loop(0, y + 1, weights_of, jnp.zeros((1, 2048), F32))
        row_max[g] = 1.0 / sums
        dq_acc[g] = jnp.zeros((128, 2048), F32)

    def grads_of(g, j):
        rows = part(j, 256, 256)
        keys, values = kb[g, rows, :], vb[g, rows, :]
        grad, query = heads_of(gb, g), heads_of(qb, g)
        prob_grad = dot(values, grad, 1, 1)
        prob = scores[g, rows, :] * row_max[g]
        score_grad = (prob * (prob_grad - delta_rows[g])).astype(BF)
        value_sum = dot(prob.astype(BF), grad, 1, 0)
        key_sum = dot(score_grad, query, 1, 0)
        dq_acc[g] = dq_acc[g] + dot(keys.T, score_grad, 1, 0)
        return key_sum * SCALE, value_sum

    def grads_copy(g, j):
        return remote(
            grads_out.at[g, j], grads_in.at[g, y], gr_s.at[j], gr_r.at[y], at(x, j, z, c)
        )

    def other_grads(g, carry):
        all_weights(g)
        arrived(gb.at[other_rows, span_of(g)], sib_r.at[2 + g])
        arrived(deltas.at[4 + 2 * oc + g], sib_r.at[4 + g])
        arrived(vb.at[g, sib_rows], kv_r.at[g, 1, y])
        mine = deltas[2 * c + g]
        theirs = deltas[4 + 2 * oc + g]
        low_half = jnp.where(c == 0, mine, theirs)
        high_half = jnp.where(c == 0, theirs, mine)
        for h in range(8):
            delta_rows[g, :, h * 256:h * 256 + 128] = low_half[h:h + 1]
            delta_rows[g, :, h * 256 + 128:(h + 1) * 256] = high_half[h:h + 1]

        def far_grads(j, inner):
            arrived(vb.at[g, part(j, 256, 256)], kv_r.at[g, 1, j])
            key_sum, value_sum = grads_of(g, j)
            grads_out[g, j, 0] = key_sum.astype(BF)
            grads_out[g, j, 1] = value_sum.astype(BF)
            grads_copy(g, j).start()
            return inner

        lax.fori_loop(0, y, far_grads, 0)
        return carry

    lax.fori_loop(0, 2, other_grads, 0)

    def last_grads(g, carry):
        key_sum, value_sum = grads_of(g, y)
        own_grads[g, 0] = key_sum
        own_grads[g, 1] = value_sum
        return carry

    lax.fori_loop(0, 2, last_grads, 0)
    for g in range(2):
        for h in range(8):
            first = (g * 8 + h) * 128
            dq_rows[:, first:first + 128] = (
                dq_acc[g, :, h * 256:(h + 1) * 256].T * SCALE
            ).astype(BF)

    arrived(down_act.at[other_rows], sib_r.at[6])

    def put_tiles(term, first):
        for k in range(NY):
            for t in range(term.shape[1] // 128):
                up_part[k, first + t] = term[k * 16:(k + 1) * 16, t * 128:(t + 1) * 128]

    def send_group(e):
        tiles = pl.ds(e * 5, 5)
        for d in range(1, NY):
            yy = (y + d) % NY
            send(up_part.at[yy, tiles], up_y.at[y, tiles], uy_s.at[0], uy_r.at[e],
                 at(x, yy, z, c))

    put_tiles(dot(down_act[:, 0:64], dq_rows[...], 0, 0).astype(BF), 0)
    for e in range(3):
        send_group(e)
    c_wq.wait()
    mid_part[:, 0:64] = dot(dq_rows[...], wq[...], 1, 1)

    c_wk.wait()
    c_wv.wait()
    def add_later(yy):
        arrived(grads_in.at[:, yy], gr_r.at[yy])
        for g in range(2):
            for which in range(2):
                own_grads[g, which] = own_grads[g, which] + grads_in[g, yy, which].astype(F32)

    each_later(add_later)
    for g in range(2):
        for which in range(2):
            kv_rows[which, :, g * 128:(g + 1) * 128] = own_grads[g, which].astype(BF)
    for which in range(2):
        weight = (wk, wv)[which]
        mid_part[:, 64 + 64 * which:128 + 64 * which] = dot(kv_rows[which], weight[...], 1, 1)
    send(mid_part, mid_sib, sib_s.at[11], sib_r.at[11], sibling, True)
    for which in range(2):
        act = down_act[:, 64 + 64 * which:128 + 64 * which]
        put_tiles(dot(act, kv_rows[which], 0, 0).astype(BF), 16 + 2 * which)
    send_group(3)

    arrived(mid_sib, sib_r.at[11])
    mid_all[part(x, 256, 256), :] = (mid_part[...] + mid_sib[...]).astype(BF)
    mid_rows = part(x * 2 + c, 128, 128)
    for d in range(1, NX):
        xx = (x + d) % NX
        send(mid_all.at[mid_rows], mid_all.at[mid_rows], mid_s.at[0], mid_r.at[x], at(xx, y, z, c))

    for g in range(2):
        span = slice(g * 1024, (g + 1) * 1024)
        there = part(c * 2 + g, 1024, 1024)
        local(dq_rows.at[my_rows, span], dq_out.at[0, :, there], 14 + g)
        send(dq_rows.at[other_rows, span], dq_out.at[0, :, there], sib_s.at[7 + g], sib_r.at[7 + g], sibling, True)
    there = part(c, 256, 256)
    for which, out in ((0, dk_out), (1, dv_out)):
        local(kv_rows.at[which, my_rows], out.at[0, :, there], 16 + which)
        send(kv_rows.at[which, other_rows], out.at[0, :, there],
             sib_s.at[9 + which], sib_r.at[9 + which], sibling, True)

    def owner_of(k):
        return (k // 5) * NZ + k % 5

    def to_owner(k):
        return remote(
            up_sum.at[k], up_rs.at[dp], us_s.at[0], us_r.at[0], {"dp": owner_of(k), "seq": seq}
        )

    def send_tile(k, carry):
        @pl.when(owner_of(k) != dp)
        def _():
            to_owner(k).start()
        return carry

    for e in range(4):
        tiles = pl.ds(e * 5, 5)
        up_y[y, tiles] = up_part[y, tiles]
        arrived(up_y.at[0:NY - 1, tiles], uy_r.at[e])
        first, second = up_y[0, tiles].astype(F32), up_y[1, tiles].astype(F32)
        third, fourth = up_y[2, tiles].astype(F32), up_y[3, tiles].astype(F32)
        up_sum[tiles] = ((first + second) + (third + fourth)).astype(BF)
        lax.fori_loop(e * 5, e * 5 + 5, send_tile, 0)

    c_xc.wait()
    for d in range(1, NX):
        xx = (x + d) % NX
        rows = part(xx * 2 + c, 128, 128)
        arrived(mid_all.at[rows], mid_r.at[xx])
        send(mid_all.at[rows], mid_all.at[rows], fwd_s.at[0], fwd_r.at[0], sibling)
    arrived(xcols.at[0:128 * (2 * NX - 1)], x_r.at[0])
    arrived(mid_all.at[0:128 * (NX - 1)], fwd_r.at[0])
    mids = mid_all[...]
    for zz in range(4):
        found = dot(mids, xcols[:, zz * 256:(zz + 1) * 256], 0, 0).T
        for yy in range(NY):
            down_part[yy, zz] = found[yy * 64:(yy + 1) * 64, :].astype(BF)
        for d in range(1, NY):
            yy = (y + d) % NY
            send(down_part.at[yy, zz], down_y.at[y, zz], dy_s.at[0], dy_r.at[zz],
                 at(x, yy, z, c))

    own_tile = x * 5 + z
    owns = z < 5

    def final_copy(d):
        other = (dp + d) % (NX * NZ)
        return remote(
            up_fin.at[own_tile], up_fin.at[own_tile], ag_s.at[0], ag_r.at[x],
            {"dp": other, "seq": seq},
        )

    @pl.when(owns)
    def _():
        up_rs[dp] = up_sum[own_tile]

        arrived(up_rs.at[0:NX * NZ - 1], us_r.at[0])
        tile = jnp.sum(up_rs[...].astype(F32), axis=0)
        up_fin[own_tile] = (tile * FACTOR).astype(BF)

        def send_one(d, carry):
            final_copy(d).start()
            return carry

        lax.fori_loop(1, NX * NZ, send_one, 0)

    def down_copy(k, cc):
        return remote(
            down_z.at[k, cc * 32:(cc + 1) * 32], down_zin.at[z], dz_s.at[0], dz_r.at[0],
            at(x, y, 4 * c + k, cc),
        )

    for k in range(4):
        down_y[y, k] = down_part[y, k]
        arrived(down_y.at[0:NY - 1, k], dy_r.at[k])
        first, second = down_y[0, k].astype(F32), down_y[1, k].astype(F32)
        third, fourth = down_y[2, k].astype(F32), down_y[3, k].astype(F32)
        down_z[k] = ((first + second) + (third + fourth)).astype(BF)
        for cc in range(2):
            @pl.when(jnp.logical_or(4 * c + k != z, cc != c))
            def _():
                down_copy(k, cc).start()

        tiles = pl.ds(k * 5, 5)
        mine = jnp.logical_and(x == k, owns)

        @pl.when(mine)
        def _():
            arrived(up_fin.at[0:4], ag_r.at[k])

        @pl.when(jnp.logical_not(mine))
        def _():
            arrived(up_fin.at[0:5], ag_r.at[k])

        for d in range(1, NY):
            yy = (y + d) % NY
            send(up_fin.at[tiles], up_out.at[c, y, tiles], ay_s.at[0], ay_r.at[k],
                 at(x, yy, z, c))
        local(up_fin.at[tiles], up_out.at[c, y, tiles], 18 + k)
        send(up_fin.at[tiles], up_out.at[c, y, tiles], sh_s.at[0], sh_r.at[0], sibling)

    source_core = z // 4

    @pl.when(source_core == c)
    def _():
        down_zin[z] = down_z[z % 4, part(c, 32, 32), :]

    @pl.when(source_core == c)
    def _():
        arrived(down_zin.at[0:NZ - 1], dz_r.at[0])

    @pl.when(source_core != c)
    def _():
        arrived(down_zin, dz_r.at[0])

    down_out[...] = jnp.sum(down_zin[...].astype(F32), axis=0) * FACTOR

    for e in range(4):
        tiles = pl.ds(e * 5, 5)
        arrived(up_out.at[c, 0:NY - 1, tiles], ay_r.at[e])
        for d in range(1, NY):
            yy = (y + d) % NY
            send(up_out.at[c, yy, tiles], up_out.at[c, yy, tiles], sh_s.at[0], sh_r.at[0], sibling)

    for copy in locals_[14:]:
        copy.wait()
    for g in range(2):
        there = part(oc * 2 + g, 1024, 1024)
        arrived(dq_out.at[0, :, there], sib_r.at[7 + g])
    there = part(oc, 256, 256)
    arrived(dk_out.at[0, :, there], sib_r.at[9])
    arrived(dv_out.at[0, :, there], sib_r.at[10])
    for copy in started:
        copy.wait_send()
    left(kb.at[:, 0:256], kv_s.at[y])

    def sent_later(yy):
        left(kb.at[:, 0:512], kv_s.at[yy])

    each_later(sent_later)

    def grads_sent(j, carry):
        left(grads_out.at[:, j], gr_s.at[j])
        return carry

    lax.fori_loop(0, y, grads_sent, 0)
    left(xcols.at[0:128 * (2 * NX - 1)], x_s.at[0])
    left(mid_all.at[0:128 * (NX - 1)], mid_s.at[0])
    left(mid_all.at[0:128 * (NX - 1)], fwd_s.at[0])
    left(down_part.at[0:NY - 1], dy_s.at[0])
    left(up_part.at[0:NY - 1], uy_s.at[0])
    left(up_out.at[c, 0:NY - 1], ay_s.at[0])
    left(up_out.at[c], sh_s.at[0])

    @pl.when(owns)
    def _():
        left(up_sum.at[0:19], us_s.at[0])
        left(up_rs.at[0:NX * NZ - 1], ag_s.at[0])

    @pl.when(jnp.logical_not(owns))
    def _():
        left(up_sum, us_s.at[0])

    @pl.when(source_core == c)
    def _():
        left(down_zin.at[0:NZ - 1], dz_s.at[0])

    @pl.when(source_core != c)
    def _():
        left(down_zin, dz_s.at[0])

    arrived(up_out.at[oc], sh_r.at[0])


def finish(
    dq_in, dk_in, dv_in, down_in, up_in, dq, dk, dv, down, upq, upk, upv,
    dq_v, dk_v, dv_v, up_v, upq_v, upk_v, upv_v, in_s, out_s,
):
    ins = [pltpu.make_async_copy(up_in, up_v, in_s.at[0])]
    outs = []
    for k in range(4):
        cols = pl.ds(k * 1024, 1024)
        ins.append(
            pltpu.make_async_copy(dq_in.at[:, :, cols], dq_v.at[:, :, cols], in_s.at[1 + k])
        )
        outs.append(pltpu.make_async_copy(dq_v.at[:, :, cols], dq.at[:, :, cols], out_s.at[k]))
    for k, (src, mid, dst) in enumerate(((dk_in, dk_v, dk), (dv_in, dv_v, dv))):
        ins.append(pltpu.make_async_copy(src, mid, in_s.at[5 + k]))
        outs.append(pltpu.make_async_copy(mid, dst, out_s.at[4 + k]))
    ups = [
        pltpu.make_async_copy(
            upq_v.at[pl.ds(k * 16, 16)], upq.at[pl.ds(k * 16, 16)], out_s.at[6 + k]
        )
        for k in range(NY)
    ]
    ups += [
        pltpu.make_async_copy(upk_v, upk, out_s.at[10]),
        pltpu.make_async_copy(upv_v, upv, out_s.at[11]),
    ]
    for copy in ins:
        copy.start()
    down[...] = down_in[...]
    for arriving, leaving in zip(ins[1:], outs):
        arriving.wait()
        leaving.start()
    ins[0].wait()
    for k in range(NY):
        rows = slice(k * 16, (k + 1) * 16)
        for cc in range(2):
            for t in range(20):
                tile = up_v[cc, k, t].astype(F32)
                if t < 16:
                    upq_v[rows, cc * 2048 + t * 128:cc * 2048 + (t + 1) * 128] = tile
                else:
                    first = cc * 256 + (t % 2) * 128
                    (upk_v if t < 18 else upv_v)[rows, first:first + 128] = tile
        ups[k].start()
    for copy in ups[4:]:
        copy.start()
    for copy in outs + ups:
        copy.wait()


def body(x_in, q_in, k_in, v_in, o_in, g_in, wd, wq, wk, wv):
    vm = pltpu.VMEM
    dma = pltpu.SemaphoreType.DMA
    any_ = pl.BlockSpec(memory_space=pl.ANY)
    vmem = pl.BlockSpec(memory_space=pltpu.VMEM)
    shape = jax.ShapeDtypeStruct
    scratch = [
        vm((128, 8192), BF), vm((192, 8192), BF), vm((64, 2048), BF), vm((64, 256), BF),
        vm((64, 256), BF), vm((256, 2048), BF), vm((256, 2048), BF), vm((2, 1024, 128), BF),
        vm((2, 1024, 128), BF), vm((128, 4096), BF), vm((128, 4096), BF), vm((8, 8, 128), F32),
        vm((256, 192), BF),
        vm((1024, 1024), BF), vm((2, 1024, 2048), F32), vm((2, 1, 2048), F32),
        vm((2, 1, 2048), F32),
        vm((2, 128, 2048), F32),
        vm((256, 2048), BF), vm((2, 4, 2, 256, 128), BF), vm((2, 4, 2, 256, 128), BF),
        vm((2, 2, 256, 128), F32),
        vm((2, 256, 256), BF), vm((256, 192), F32), vm((256, 192), F32), vm((1024, 192), BF),
        vm((4, 4, 64, 192), BF), vm((4, 4, 64, 192), BF), vm((4, 64, 192), BF), vm((8, 32, 192), BF),
        vm((4, 20, 16, 128), BF), vm((4, 20, 16, 128), BF), vm((20, 16, 128), BF),
        vm((32, 16, 128), BF), vm((20, 16, 128), BF),
        dma((22,)), dma((12,)), dma((12,)), dma((4,)), dma((2, 2, 4)), dma((1,)), dma((1,)),
        dma((4,)), dma((4,)), dma((1,)), dma((4,)), dma((1,)), dma((1,)),
        dma((1,)), dma((4,)), dma((1,)), dma((1,)), dma((1,)), dma((4,)), dma((1,)), dma((1,)),
        dma((1,)), dma((4,)), dma((1,)), dma((4,)), dma((1,)), dma((1,)),
    ]
    first = pl.pallas_call(
        kernel,
        out_shape=[
            shape((1, 128, 4096), BF), shape((1, 128, 512), BF), shape((1, 128, 512), BF),
            shape((32, 192), F32), shape((2, 4, 20, 16, 128), BF),
        ],
        in_specs=[any_] * 10,
        out_specs=[any_] * 3 + [vmem, any_],
        scratch_shapes=scratch,
        compiler_params=pltpu.CompilerParams(
            vmem_limit_bytes=60 * 2**20, collective_id=0, has_side_effects=True
        ),
        cost_estimate=pl.CostEstimate(
            flops=8 * 10**9, bytes_accessed=12 * 2**20, transcendentals=4 * 2**20
        ),
    )(x_in, q_in, k_in, v_in, o_in, g_in, wd.T, wq, wk, wv)
    return pl.pallas_call(
        finish,
        out_shape=[
            shape((1, 128, 4096), BF), shape((1, 128, 512), BF), shape((1, 128, 512), BF),
            shape((32, 192), F32), shape((64, 4096), F32), shape((64, 512), F32),
            shape((64, 512), F32),
        ],
        in_specs=[any_] * 3 + [vmem, any_],
        out_specs=[any_] * 3 + [vmem] + [any_] * 3,
        scratch_shapes=[
            vm((1, 128, 4096), BF), vm((1, 128, 512), BF), vm((1, 128, 512), BF),
            vm((2, 4, 20, 16, 128), BF), vm((64, 4096), F32), vm((64, 512), F32),
            vm((64, 512), F32), dma((7,)), dma((12,)),
        ],
        compiler_params=pltpu.CompilerParams(vmem_limit_bytes=60 * 2**20),
        cost_estimate=pl.CostEstimate(flops=10**6, bytes_accessed=6 * 2**20, transcendentals=0),
    )(*first)


def solution(mesh):
    token = P("dp", "seq", None)
    return jax.shard_map(
        body,
        mesh=mesh,
        in_specs=(token,) * 6 + (P(),) * 4,
        out_specs=(token,) * 3 + (P(("dp", "seq"), None), P(), P(), P()),
        check_vma=False,
    )
```

```python
import math

import jax
import jax.numpy as jnp
from jax import lax
from jax.experimental import pallas as pl
from jax.experimental.pallas import tpu as pltpu
from jax.sharding import PartitionSpec as P

BF = jnp.bfloat16
F32 = jnp.float32
HEAD = 128
SCALE = HEAD**-0.5
LOG2_SCALE = SCALE * math.log2(math.e)
FACTOR = 0.25 / math.sqrt(32768)
NX, NY, NZ = 4, 4, 8
ROWS = 2048


def dot(left, right, left_axis, right_axis):
    return lax.dot_general(
        left, right, (((left_axis,), (right_axis,)), ((), ())), preferred_element_type=F32
    )


def kernel(
    x_in, q_in, k_in, v_in, o_in, g_in, wd_in, wq_in, wk_in, wv_in,
    dq_out, dk_out, dv_out, down_out, up_out,
    xv, wd, wq, wk, wv, qb, gb, kb, vb, gown, oown, deltas, down_act,
    xcols, scores, row_max, delta_rows, dq_acc, dq_rows, grads_out, grads_in, own_grads,
    kv_rows, mid_part, mid_sib, mid_all, down_part, down_y, down_z, down_zin, down_sum,
    up_part, up_y, up_sum, up_rs, up_fin,
    loc, sib_s, sib_r, kv_s, kv_r, x_s, x_r, gr_s, gr_r, mid_s, mid_r, fwd_s, fwd_r,
    dy_s, dy_r, dz_s, dz_r, uy_s, uy_r, us_s, us_r, ag_s, ag_r, ay_s, ay_r, sh_s, sh_r,
):
    dp = lax.axis_index("dp")
    seq = lax.axis_index("seq")
    x, z = dp // NZ, dp % NZ
    y, c = seq // 2, seq % 2
    oc = 1 - c

    def at(xx, yy, zz, cc):
        return {"dp": xx * NZ + zz, "seq": yy * 2 + cc}

    sibling = at(x, y, z, oc)

    def remote(src, dst, ssem, rsem, device):
        return pltpu.make_async_remote_copy(
            src_ref=src, dst_ref=dst, send_sem=ssem, recv_sem=rsem,
            device_id=device, device_id_type=pl.DeviceIdType.MESH,
        )

    def arrived(dst, rsem):
        remote(dst, dst, sib_s.at[0], rsem, sibling).wait_recv()

    def left(src, ssem):
        remote(src, src, ssem, sib_r.at[0], sibling).wait_send()

    def part(start, size, unit):
        return pl.ds(pl.multiple_of(start * unit, unit), size)

    locals_ = []

    def local(src, dst, index):
        copy = pltpu.make_async_copy(src, dst, loc.at[index])
        copy.start()
        locals_.append(copy)
        return copy

    my_rows = part(c, 128, 128)
    c_gown = local(g_in.at[0], gown, 0)
    c_oown = local(o_in.at[0], oown, 1)
    c_q = local(q_in.at[0, :, part(c, 2048, 2048)], qb.at[my_rows], 2)
    c_g = local(g_in.at[0, :, part(c, 2048, 2048)], gb.at[my_rows], 3)
    chip_rows = part(seq, 128, 128)
    c_kv = []
    for g in range(2):
        head = part(2 * c + g, 128, 128)
        c_kv.append((
            local(k_in.at[0, :, head], kb.at[g, chip_rows], 4 + 2 * g),
            local(v_in.at[0, :, head], vb.at[g, chip_rows], 5 + 2 * g),
        ))
    c_x = local(x_in.at[0], xv, 8)
    c_wd = local(wd_in, wd, 9)
    c_xc = local(
        x_in.at[0, :, part(x * 2 + c, 1024, 1024)], xcols.at[part(x * 2 + c, 128, 128)], 10
    )
    c_wq = local(wq_in.at[:, part(c, 2048, 2048)], wq, 11)
    c_wk = local(wk_in.at[:, part(c, 256, 256)], wk, 12)
    c_wv = local(wv_in.at[:, part(c, 256, 256)], wv, 13)

    barrier = pltpu.get_barrier_semaphore()

    def greet(device):
        pl.semaphore_signal(
            barrier, inc=1, device_id=device, device_id_type=pl.DeviceIdType.MESH
        )

    greet(sibling)
    for d in range(1, NY):
        for cc in range(2):
            greet(at(x, (y + d) % NY, z, cc))
    for d in range(1, NX):
        greet(at((x + d) % NX, y, z, oc))
    for d in range(1, NZ):
        greet(at(x, y, (z + d) % NZ, oc))
    for d in range(1, NX * NZ):
        greet({"dp": (dp + d) % (NX * NZ), "seq": seq})
    pl.semaphore_wait(barrier, 1 + 2 * (NY - 1) + NX - 1 + NZ - 1 + NX * NZ - 1)

    started = []

    def send(src, dst, ssem, rsem, device, alone=False):
        copy = remote(src, dst, ssem, rsem, device)
        copy.start()
        if alone:
            started.append(copy)

    def kv_copy(g, which, yy, cc):
        source, target = ((k_in, kb), (v_in, vb))[which]
        return remote(
            source.at[0, :, part(2 * cc + g, 128, 128)],
            target.at[g, chip_rows],
            kv_s.at[yy],
            kv_r.at[g, which, y],
            at(x, yy, z, cc),
        )

    def each_later(body):
        for yy in range(NY - 1, 0, -1):
            @pl.when(y < yy)
            def _():
                body(yy)

    def send_kv(g, which):
        kv_copy(g, which, y, oc).start()

        def go(yy):
            for cc in range(2):
                kv_copy(g, which, yy, cc).start()

        each_later(go)

    def span_of(g):
        return part(g, 1024, 1024)

    for g in range(2):
        send(q_in.at[0, :, span_of(oc * 2 + g)], qb.at[my_rows, span_of(g)],
             sib_s.at[g], sib_r.at[g], sibling, True)
        for which in range(2):
            send_kv(g, which)
        send(g_in.at[0, :, span_of(oc * 2 + g)], gb.at[my_rows, span_of(g)],
             sib_s.at[2 + g], sib_r.at[2 + g], sibling, True)

    c_gown.wait()
    c_oown.wait()
    pick = (
        lax.broadcasted_iota(jnp.int32, (8, 1024), 1) // 128
        == lax.broadcasted_iota(jnp.int32, (8, 1024), 0)
    ).astype(BF)
    for chunk in range(4):
        cols = slice(chunk * 1024, (chunk + 1) * 1024)
        product = gown[:, cols].astype(F32) * oown[:, cols].astype(F32)
        high = product.astype(BF)
        low = (product - high.astype(F32)).astype(BF)
        deltas[chunk] = dot(pick, high, 1, 1) + dot(pick, low, 1, 1)
    for g in range(2):
        send(deltas.at[oc * 2 + g], deltas.at[4 + 2 * c + g], sib_s.at[4 + g], sib_r.at[4 + g], sibling, True)

    c_x.wait()
    c_wd.wait()
    total = jnp.zeros((128, 192), F32)
    for chunk in range(4):
        cols = slice(chunk * 2048, (chunk + 1) * 2048)
        total += dot(xv[:, cols], wd[:, cols], 1, 1)
    down_act[my_rows, :] = total.astype(BF)
    send(down_act.at[my_rows], down_act.at[my_rows], sib_s.at[6], sib_r.at[6], sibling, True)
    for d in range(NX):
        for cc in ([oc] if d == 0 else [0, 1]):
            xx = (x + d) % NX
            send(x_in.at[0, :, part(xx * 2 + cc, 1024, 1024)],
                 xcols.at[part(x * 2 + c, 128, 128)],
                 x_s.at[0], x_r.at[0], at(xx, y, z, cc))

    c_q.wait()
    c_g.wait()
    other_rows = part(oc, 128, 128)

    def heads_of(ref, g):
        return jnp.concatenate(
            [ref[:, part(g * 8 + h, 128, 128)] for h in range(8)], axis=0
        )

    sib_rows = part(y * 2 + oc, 128, 128)
    for g in range(2):
        c_kv[g][0].wait()
        c_kv[g][1].wait()

    def scores_of(g, j, first):
        rows = part(j, 256, 256)
        s = dot(kb[g, rows, :], heads_of(qb, g), 1, 1)
        if first:
            key_at = lax.broadcasted_iota(jnp.int32, (256, ROWS), 0)
            query_at = lax.broadcasted_iota(jnp.int32, (256, ROWS), 1) % 256
            s = jnp.where(key_at <= query_at, s, -jnp.inf)
        scores[g, rows, :] = s
        top = jnp.max(s, axis=0, keepdims=True)
        row_max[g] = top if first else jnp.maximum(row_max[g], top)

    def own_scores(g, carry):
        arrived(qb.at[other_rows, span_of(g)], sib_r.at[g])
        arrived(kb.at[g, sib_rows], kv_r.at[g, 0, y])
        scores_of(g, y, True)
        return carry

    lax.fori_loop(0, 2, own_scores, 0)

    def all_weights(g):
        def more_scores(t, inner):
            j = y - 1 - t
            arrived(kb.at[g, part(j, 256, 256)], kv_r.at[g, 0, j])
            scores_of(g, j, False)
            return inner

        lax.fori_loop(0, y, more_scores, 0)
        row_max[g] = row_max[g] * LOG2_SCALE

        def weights_of(j, sums):
            rows = part(j, 256, 256)
            found = []
            for h in range(0, 8, 2):
                qs = slice(h * 256, h * 256 + 512)
                w = jnp.exp2(scores[g, rows, qs] * LOG2_SCALE - row_max[g, :, qs])
                scores[g, rows, qs] = w
                found.append(jnp.sum(w, axis=0, keepdims=True))
            return sums + jnp.concatenate(found, axis=1)

        sums = lax.fori_loop(0, y + 1, weights_of, jnp.zeros((1, 2048), F32))
        row_max[g] = 1.0 / sums
        dq_acc[g] = jnp.zeros((128, 2048), F32)

    def grads_of(g, j):
        rows = part(j, 256, 256)
        keys, values = kb[g, rows, :], vb[g, rows, :]
        grad, query = heads_of(gb, g), heads_of(qb, g)
        prob_grad = dot(values, grad, 1, 1)
        prob = scores[g, rows, :] * row_max[g]
        score_grad = (prob * (prob_grad - delta_rows[g])).astype(BF)
        value_sum = dot(prob.astype(BF), grad, 1, 0)
        key_sum = dot(score_grad, query, 1, 0)
        dq_acc[g] = dq_acc[g] + dot(keys.T, score_grad, 1, 0)
        return key_sum * SCALE, value_sum

    def grads_copy(g, j):
        return remote(
            grads_out.at[g, j], grads_in.at[g, y], gr_s.at[j], gr_r.at[y], at(x, j, z, c)
        )

    def other_grads(g, carry):
        all_weights(g)
        arrived(gb.at[other_rows, span_of(g)], sib_r.at[2 + g])
        arrived(deltas.at[4 + 2 * oc + g], sib_r.at[4 + g])
        arrived(vb.at[g, sib_rows], kv_r.at[g, 1, y])
        mine = deltas[2 * c + g]
        theirs = deltas[4 + 2 * oc + g]
        low_half = jnp.where(c == 0, mine, theirs)
        high_half = jnp.where(c == 0, theirs, mine)
        for h in range(8):
            delta_rows[g, :, h * 256:h * 256 + 128] = low_half[h:h + 1]
            delta_rows[g, :, h * 256 + 128:(h + 1) * 256] = high_half[h:h + 1]

        def far_grads(j, inner):
            arrived(vb.at[g, part(j, 256, 256)], kv_r.at[g, 1, j])
            key_sum, value_sum = grads_of(g, j)
            grads_out[g, j, 0] = key_sum.astype(BF)
            grads_out[g, j, 1] = value_sum.astype(BF)
            grads_copy(g, j).start()
            return inner

        lax.fori_loop(0, y, far_grads, 0)
        return carry

    lax.fori_loop(0, 2, other_grads, 0)

    def last_grads(g, carry):
        key_sum, value_sum = grads_of(g, y)
        own_grads[g, 0] = key_sum
        own_grads[g, 1] = value_sum
        return carry

    lax.fori_loop(0, 2, last_grads, 0)
    for g in range(2):
        for h in range(8):
            first = (g * 8 + h) * 128
            dq_rows[:, first:first + 128] = (
                dq_acc[g, :, h * 256:(h + 1) * 256].T * SCALE
            ).astype(BF)

    arrived(down_act.at[other_rows], sib_r.at[6])

    def put_tiles(term, first):
        for k in range(NY):
            for t in range(term.shape[1] // 128):
                up_part[k, first + t] = term[k * 16:(k + 1) * 16, t * 128:(t + 1) * 128]

    def send_group(e):
        tiles = pl.ds(e * 5, 5)
        for d in range(1, NY):
            yy = (y + d) % NY
            send(up_part.at[yy, tiles], up_y.at[y, tiles], uy_s.at[0], uy_r.at[e],
                 at(x, yy, z, c))

    put_tiles(dot(down_act[:, 0:64], dq_rows[...], 0, 0).astype(BF), 0)
    for e in range(3):
        send_group(e)
    c_wq.wait()
    mid_part[:, 0:64] = dot(dq_rows[...], wq[...], 1, 1)

    c_wk.wait()
    c_wv.wait()
    def add_later(yy):
        arrived(grads_in.at[:, yy], gr_r.at[yy])
        for g in range(2):
            for which in range(2):
                own_grads[g, which] = own_grads[g, which] + grads_in[g, yy, which].astype(F32)

    each_later(add_later)
    for g in range(2):
        for which in range(2):
            kv_rows[which, :, g * 128:(g + 1) * 128] = own_grads[g, which].astype(BF)
    for which in range(2):
        weight = (wk, wv)[which]
        mid_part[:, 64 + 64 * which:128 + 64 * which] = dot(kv_rows[which], weight[...], 1, 1)
    send(mid_part, mid_sib, sib_s.at[11], sib_r.at[11], sibling, True)
    for which in range(2):
        act = down_act[:, 64 + 64 * which:128 + 64 * which]
        put_tiles(dot(act, kv_rows[which], 0, 0).astype(BF), 16 + 2 * which)
    send_group(3)

    arrived(mid_sib, sib_r.at[11])
    mid_all[part(x, 256, 256), :] = (mid_part[...] + mid_sib[...]).astype(BF)
    mid_rows = part(x * 2 + c, 128, 128)
    for d in range(1, NX):
        xx = (x + d) % NX
        send(mid_all.at[mid_rows], mid_all.at[mid_rows], mid_s.at[0], mid_r.at[x], at(xx, y, z, c))

    for g in range(2):
        span = slice(g * 1024, (g + 1) * 1024)
        there = part(c * 2 + g, 1024, 1024)
        local(dq_rows.at[my_rows, span], dq_out.at[0, :, there], 14 + g)
        send(dq_rows.at[other_rows, span], dq_out.at[0, :, there], sib_s.at[7 + g], sib_r.at[7 + g], sibling, True)
    there = part(c, 256, 256)
    for which, out in ((0, dk_out), (1, dv_out)):
        local(kv_rows.at[which, my_rows], out.at[0, :, there], 16 + which)
        send(kv_rows.at[which, other_rows], out.at[0, :, there],
             sib_s.at[9 + which], sib_r.at[9 + which], sibling, True)

    def owner_of(k):
        return (k // 5) * NZ + k % 5

    def to_owner(k):
        return remote(
            up_sum.at[k], up_rs.at[dp], us_s.at[0], us_r.at[0], {"dp": owner_of(k), "seq": seq}
        )

    def send_tile(k, carry):
        @pl.when(owner_of(k) != dp)
        def _():
            to_owner(k).start()
        return carry

    for e in range(4):
        tiles = pl.ds(e * 5, 5)
        up_y[y, tiles] = up_part[y, tiles]
        arrived(up_y.at[0:NY - 1, tiles], uy_r.at[e])
        first, second = up_y[0, tiles].astype(F32), up_y[1, tiles].astype(F32)
        third, fourth = up_y[2, tiles].astype(F32), up_y[3, tiles].astype(F32)
        up_sum[tiles] = ((first + second) + (third + fourth)).astype(BF)
        lax.fori_loop(e * 5, e * 5 + 5, send_tile, 0)

    own_tile = x * 5 + z
    owns = z < 5

    def final_copy(d):
        other = (dp + d) % (NX * NZ)
        return remote(
            up_fin.at[own_tile], up_fin.at[own_tile], ag_s.at[0], ag_r.at[x],
            {"dp": other, "seq": seq},
        )

    @pl.when(owns)
    def _():
        up_rs[dp] = up_sum[own_tile]

        arrived(up_rs.at[0:NX * NZ - 1], us_r.at[0])
        tile = jnp.sum(up_rs[...].astype(F32), axis=0)
        up_fin[own_tile] = (tile * FACTOR).astype(BF)

        def send_one(d, carry):
            final_copy(d).start()
            return carry

        lax.fori_loop(1, NX * NZ, send_one, 0)

    c_xc.wait()
    for d in range(1, NX):
        xx = (x + d) % NX
        rows = part(xx * 2 + c, 128, 128)
        arrived(mid_all.at[rows], mid_r.at[xx])
        send(mid_all.at[rows], mid_all.at[rows], fwd_s.at[0], fwd_r.at[0], sibling)
    arrived(xcols.at[0:128 * (2 * NX - 1)], x_r.at[0])
    arrived(mid_all.at[0:128 * (NX - 1)], fwd_r.at[0])
    mids = mid_all[...]
    for p in range(2):
        blocks = [
            dot(mids, xcols[:, zz * 256:(zz + 1) * 256], 0, 0) for zz in (2 * p, 2 * p + 1)
        ]
        packed = [found[0:128].T for found in blocks]
        packed.append(jnp.concatenate([found[128:192] for found in blocks], axis=0).T)
        for yy in range(NY):
            for k in range(3):
                down_part[yy, p, k] = packed[k][yy * 64:(yy + 1) * 64, :].astype(BF)
        for d in range(1, NY):
            yy = (y + d) % NY
            send(down_part.at[yy, p], down_y.at[y, p], dy_s.at[0], dy_r.at[p], at(x, yy, z, c))

    def down_copy(k, cc):
        return remote(
            down_z.at[k, cc * 32:(cc + 1) * 32], down_zin.at[z], dz_s.at[0], dz_r.at[0],
            at(x, y, 4 * c + k, cc),
        )

    for k in range(4):
        if k % 2 == 0:
            p = k // 2
            down_y[y, p] = down_part[y, p]
            arrived(down_y.at[0:NY - 1, p], dy_r.at[p])
            first, second = down_y[0, p].astype(F32), down_y[1, p].astype(F32)
            third, fourth = down_y[2, p].astype(F32), down_y[3, p].astype(F32)
            summed = (first + second) + (third + fourth)
            for i in range(2):
                down_z[k + i] = jnp.concatenate(
                    [summed[i], summed[2][:, i * 64:(i + 1) * 64]], axis=1
                ).astype(BF)
        for cc in range(2):
            @pl.when(jnp.logical_or(4 * c + k != z, cc != c))
            def _():
                down_copy(k, cc).start()

        tiles = pl.ds(k * 5, 5)
        mine = jnp.logical_and(x == k, owns)

        @pl.when(mine)
        def _():
            arrived(up_fin.at[0:4], ag_r.at[k])

        @pl.when(jnp.logical_not(mine))
        def _():
            arrived(up_fin.at[0:5], ag_r.at[k])

        for d in range(1, NY):
            yy = (y + d) % NY
            send(up_fin.at[tiles], up_out.at[c, y, tiles], ay_s.at[0], ay_r.at[k],
                 at(x, yy, z, c))
        local(up_fin.at[tiles], up_out.at[c, y, tiles], 18 + k)
        send(up_fin.at[tiles], up_out.at[c, y, tiles], sh_s.at[0], sh_r.at[0], sibling)

    source_core = z // 4

    @pl.when(source_core == c)
    def _():
        down_zin[z] = down_z[z % 4, part(c, 32, 32), :]

    @pl.when(source_core == c)
    def _():
        arrived(down_zin.at[0:NZ - 1], dz_r.at[0])

    @pl.when(source_core != c)
    def _():
        arrived(down_zin, dz_r.at[0])

    down_sum[...] = jnp.sum(down_zin[...].astype(F32), axis=0) * FACTOR
    local(down_sum, down_out, 22)

    for e in range(4):
        tiles = pl.ds(e * 5, 5)
        arrived(up_out.at[c, 0:NY - 1, tiles], ay_r.at[e])
        for d in range(1, NY):
            yy = (y + d) % NY
            send(up_out.at[c, yy, tiles], up_out.at[c, yy, tiles], sh_s.at[0], sh_r.at[0], sibling)

    for copy in locals_[14:]:
        copy.wait()
    for g in range(2):
        there = part(oc * 2 + g, 1024, 1024)
        arrived(dq_out.at[0, :, there], sib_r.at[7 + g])
    there = part(oc, 256, 256)
    arrived(dk_out.at[0, :, there], sib_r.at[9])
    arrived(dv_out.at[0, :, there], sib_r.at[10])
    for copy in started:
        copy.wait_send()
    left(kb.at[:, 0:256], kv_s.at[y])

    def sent_later(yy):
        left(kb.at[:, 0:512], kv_s.at[yy])

    each_later(sent_later)

    def grads_sent(j, carry):
        left(grads_out.at[:, j], gr_s.at[j])
        return carry

    lax.fori_loop(0, y, grads_sent, 0)
    left(xcols.at[0:128 * (2 * NX - 1)], x_s.at[0])
    left(mid_all.at[0:128 * (NX - 1)], mid_s.at[0])
    left(mid_all.at[0:128 * (NX - 1)], fwd_s.at[0])
    left(down_part.at[0:NY - 1], dy_s.at[0])
    left(up_part.at[0:NY - 1], uy_s.at[0])
    left(up_out.at[c, 0:NY - 1], ay_s.at[0])
    left(up_out.at[c], sh_s.at[0])

    @pl.when(owns)
    def _():
        left(up_sum.at[0:19], us_s.at[0])
        left(up_rs.at[0:NX * NZ - 1], ag_s.at[0])

    @pl.when(jnp.logical_not(owns))
    def _():
        left(up_sum, us_s.at[0])

    @pl.when(source_core == c)
    def _():
        left(down_zin.at[0:NZ - 1], dz_s.at[0])

    @pl.when(source_core != c)
    def _():
        left(down_zin, dz_s.at[0])

    arrived(up_out.at[oc], sh_r.at[0])


def finish(
    dq_in, dk_in, dv_in, down_in, up_in, dq, dk, dv, down, upq, upk, upv,
    dq_v, dk_v, dv_v, down_v, up_v, upq_v, upk_v, upv_v, in_s, out_s,
):
    ins = [pltpu.make_async_copy(up_in, up_v, in_s.at[0])]
    outs = []
    for k in range(4):
        cols = pl.ds(k * 1024, 1024)
        ins.append(
            pltpu.make_async_copy(dq_in.at[:, :, cols], dq_v.at[:, :, cols], in_s.at[1 + k])
        )
        outs.append(pltpu.make_async_copy(dq_v.at[:, :, cols], dq.at[:, :, cols], out_s.at[k]))
    for k, (src, mid, dst) in enumerate(
        ((dk_in, dk_v, dk), (dv_in, dv_v, dv), (down_in, down_v, down))
    ):
        ins.append(pltpu.make_async_copy(src, mid, in_s.at[5 + k]))
        outs.append(pltpu.make_async_copy(mid, dst, out_s.at[4 + k]))
    ups = [
        pltpu.make_async_copy(
            upq_v.at[pl.ds(k * 16, 16)], upq.at[pl.ds(k * 16, 16)], out_s.at[7 + k]
        )
        for k in range(NY)
    ]
    ups += [
        pltpu.make_async_copy(upk_v, upk, out_s.at[11]),
        pltpu.make_async_copy(upv_v, upv, out_s.at[12]),
    ]
    for copy in ins:
        copy.start()
    for arriving, leaving in zip(ins[1:], outs):
        arriving.wait()
        leaving.start()
    ins[0].wait()
    for k in range(NY):
        rows = slice(k * 16, (k + 1) * 16)
        for cc in range(2):
            for t in range(20):
                tile = up_v[cc, k, t].astype(F32)
                if t < 16:
                    upq_v[rows, cc * 2048 + t * 128:cc * 2048 + (t + 1) * 128] = tile
                else:
                    first = cc * 256 + (t % 2) * 128
                    (upk_v if t < 18 else upv_v)[rows, first:first + 128] = tile
        ups[k].start()
    for copy in ups[4:]:
        copy.start()
    for copy in outs + ups:
        copy.wait()


def body(x_in, q_in, k_in, v_in, o_in, g_in, wd, wq, wk, wv):
    vm = pltpu.VMEM
    dma = pltpu.SemaphoreType.DMA
    any_ = pl.BlockSpec(memory_space=pl.ANY)
    shape = jax.ShapeDtypeStruct
    scratch = [
        vm((128, 8192), BF), vm((192, 8192), BF), vm((64, 2048), BF), vm((64, 256), BF),
        vm((64, 256), BF), vm((256, 2048), BF), vm((256, 2048), BF), vm((2, 1024, 128), BF),
        vm((2, 1024, 128), BF), vm((128, 4096), BF), vm((128, 4096), BF), vm((8, 8, 128), F32),
        vm((256, 192), BF),
        vm((1024, 1024), BF), vm((2, 1024, 2048), F32), vm((2, 1, 2048), F32),
        vm((2, 1, 2048), F32),
        vm((2, 128, 2048), F32),
        vm((256, 2048), BF), vm((2, 4, 2, 256, 128), BF), vm((2, 4, 2, 256, 128), BF),
        vm((2, 2, 256, 128), F32),
        vm((2, 256, 256), BF), vm((256, 192), F32), vm((256, 192), F32), vm((1024, 192), BF),
        vm((4, 2, 3, 64, 128), BF), vm((4, 2, 3, 64, 128), BF), vm((4, 64, 192), BF), vm((8, 32, 192), BF),
        vm((32, 192), F32),
        vm((4, 20, 16, 128), BF), vm((4, 20, 16, 128), BF), vm((20, 16, 128), BF),
        vm((32, 16, 128), BF), vm((20, 16, 128), BF),
        dma((23,)), dma((12,)), dma((12,)), dma((4,)), dma((2, 2, 4)), dma((1,)), dma((1,)),
        dma((4,)), dma((4,)), dma((1,)), dma((4,)), dma((1,)), dma((1,)),
        dma((1,)), dma((4,)), dma((1,)), dma((1,)), dma((1,)), dma((4,)), dma((1,)), dma((1,)),
        dma((1,)), dma((4,)), dma((1,)), dma((4,)), dma((1,)), dma((1,)),
    ]
    first = pl.pallas_call(
        kernel,
        out_shape=[
            shape((1, 128, 4096), BF), shape((1, 128, 512), BF), shape((1, 128, 512), BF),
            shape((32, 192), F32), shape((2, 4, 20, 16, 128), BF),
        ],
        in_specs=[any_] * 10,
        out_specs=[any_] * 5,
        scratch_shapes=scratch,
        compiler_params=pltpu.CompilerParams(
            vmem_limit_bytes=60 * 2**20, collective_id=0, has_side_effects=True
        ),
        cost_estimate=pl.CostEstimate(
            flops=8 * 10**9, bytes_accessed=12 * 2**20, transcendentals=4 * 2**20
        ),
    )(x_in, q_in, k_in, v_in, o_in, g_in, wd.T, wq, wk, wv)
    return pl.pallas_call(
        finish,
        out_shape=[
            shape((1, 128, 4096), BF), shape((1, 128, 512), BF), shape((1, 128, 512), BF),
            shape((32, 192), F32), shape((64, 4096), F32), shape((64, 512), F32),
            shape((64, 512), F32),
        ],
        in_specs=[any_] * 5,
        out_specs=[any_] * 7,
        scratch_shapes=[
            vm((1, 128, 4096), BF), vm((1, 128, 512), BF), vm((1, 128, 512), BF),
            vm((32, 192), F32), vm((2, 4, 20, 16, 128), BF), vm((64, 4096), F32),
            vm((64, 512), F32), vm((64, 512), F32), dma((8,)), dma((13,)),
        ],
        compiler_params=pltpu.CompilerParams(vmem_limit_bytes=60 * 2**20),
        cost_estimate=pl.CostEstimate(flops=10**6, bytes_accessed=6 * 2**20, transcendentals=0),
    )(*first)


def solution(mesh):
    token = P("dp", "seq", None)
    return jax.shard_map(
        body,
        mesh=mesh,
        in_specs=(token,) * 6 + (P(),) * 4,
        out_specs=(token,) * 3 + (P(("dp", "seq"), None), P(), P(), P()),
        check_vma=False,
    )
```

```python
import math

import jax
import jax.numpy as jnp
from jax import lax
from jax.experimental import pallas as pl
from jax.experimental.pallas import tpu as pltpu
from jax.sharding import PartitionSpec as P

BF = jnp.bfloat16
F32 = jnp.float32
HEAD = 128
SCALE = HEAD**-0.5
LOG2_SCALE = SCALE * math.log2(math.e)
FACTOR = 0.25 / math.sqrt(32768)
NX, NY, NZ = 4, 4, 8
ROWS = 2048


def dot(left, right, left_axis, right_axis):
    return lax.dot_general(
        left, right, (((left_axis,), (right_axis,)), ((), ())), preferred_element_type=F32
    )


def kernel(
    x_in, q_in, k_in, v_in, o_in, g_in, wd_in, wq_in, wk_in, wv_in,
    dq_out, dk_out, dv_out, down_out, up_out,
    xv, wd, wq, wk, wv, qb, gb, kb, vb, gown, oown, deltas, down_act,
    xcols, scores, row_max, delta_rows, dq_acc, dq_rows, grads_out, grads_in, own_grads,
    kv_rows, mid_part, mid_sib, mid_all, down_part, down_y, down_z, down_zin, down_sum,
    up_part, up_y, up_sum, up_rs, up_fin,
    loc, sib_s, sib_r, kv_s, kv_r, x_s, x_r, gr_s, gr_r, mid_s, mid_r, fwd_s, fwd_r,
    dy_s, dy_r, dz_s, dz_r, uy_s, uy_r, us_s, us_r, ag_s, ag_r, ay_s, ay_r, sh_s, sh_r,
):
    dp = lax.axis_index("dp")
    seq = lax.axis_index("seq")
    x, z = dp // NZ, dp % NZ
    y, c = seq // 2, seq % 2
    oc = 1 - c

    def at(xx, yy, zz, cc):
        return {"dp": xx * NZ + zz, "seq": yy * 2 + cc}

    sibling = at(x, y, z, oc)

    def remote(src, dst, ssem, rsem, device):
        return pltpu.make_async_remote_copy(
            src_ref=src, dst_ref=dst, send_sem=ssem, recv_sem=rsem,
            device_id=device, device_id_type=pl.DeviceIdType.MESH,
        )

    def arrived(dst, rsem):
        remote(dst, dst, sib_s.at[0], rsem, sibling).wait_recv()

    def left(src, ssem):
        remote(src, src, ssem, sib_r.at[0], sibling).wait_send()

    def part(start, size, unit):
        return pl.ds(pl.multiple_of(start * unit, unit), size)

    locals_ = []

    def local(src, dst, index):
        copy = pltpu.make_async_copy(src, dst, loc.at[index])
        copy.start()
        locals_.append(copy)
        return copy

    my_rows = part(c, 128, 128)
    c_gown = local(g_in.at[0], gown, 0)
    c_oown = local(o_in.at[0], oown, 1)
    c_q = local(q_in.at[0, :, part(c, 2048, 2048)], qb.at[my_rows], 2)
    c_g = local(g_in.at[0, :, part(c, 2048, 2048)], gb.at[my_rows], 3)
    chip_rows = part(seq, 128, 128)
    c_kv = []
    for g in range(2):
        head = part(2 * c + g, 128, 128)
        c_kv.append((
            local(k_in.at[0, :, head], kb.at[g, chip_rows], 4 + 2 * g),
            local(v_in.at[0, :, head], vb.at[g, chip_rows], 5 + 2 * g),
        ))
    c_x = local(x_in.at[0], xv, 8)
    c_wd = local(wd_in, wd, 9)
    c_xc = local(
        x_in.at[0, :, part(x * 2 + c, 1024, 1024)], xcols.at[part(x * 2 + c, 128, 128)], 10
    )
    c_wq = local(wq_in.at[:, part(c, 2048, 2048)], wq, 11)
    c_wk = local(wk_in.at[:, part(c, 256, 256)], wk, 12)
    c_wv = local(wv_in.at[:, part(c, 256, 256)], wv, 13)

    barrier = pltpu.get_barrier_semaphore()

    def greet(device):
        pl.semaphore_signal(
            barrier, inc=1, device_id=device, device_id_type=pl.DeviceIdType.MESH
        )

    greet(sibling)
    for d in range(1, NY):
        for cc in range(2):
            greet(at(x, (y + d) % NY, z, cc))
    for d in range(1, NX):
        greet(at((x + d) % NX, y, z, oc))
    for d in range(1, NZ):
        greet(at(x, y, (z + d) % NZ, oc))
    for d in range(1, NX * NZ):
        greet({"dp": (dp + d) % (NX * NZ), "seq": seq})
    pl.semaphore_wait(barrier, 1 + 2 * (NY - 1) + NX - 1 + NZ - 1 + NX * NZ - 1)

    started = []

    def send(src, dst, ssem, rsem, device, alone=False):
        copy = remote(src, dst, ssem, rsem, device)
        copy.start()
        if alone:
            started.append(copy)

    def kv_copy(g, which, yy, cc):
        source, target = ((k_in, kb), (v_in, vb))[which]
        return remote(
            source.at[0, :, part(2 * cc + g, 128, 128)],
            target.at[g, chip_rows],
            kv_s.at[yy],
            kv_r.at[g, which, y],
            at(x, yy, z, cc),
        )

    def each_later(body):
        for yy in range(NY - 1, 0, -1):
            @pl.when(y < yy)
            def _():
                body(yy)

    def send_kv(g, which):
        kv_copy(g, which, y, oc).start()

        def go(yy):
            for cc in range(2):
                kv_copy(g, which, yy, cc).start()

        each_later(go)

    def span_of(g):
        return part(g, 1024, 1024)

    for g in range(2):
        send(q_in.at[0, :, span_of(oc * 2 + g)], qb.at[my_rows, span_of(g)],
             sib_s.at[g], sib_r.at[g], sibling, True)
        for which in range(2):
            send_kv(g, which)
        send(g_in.at[0, :, span_of(oc * 2 + g)], gb.at[my_rows, span_of(g)],
             sib_s.at[2 + g], sib_r.at[2 + g], sibling, True)

    c_gown.wait()
    c_oown.wait()
    pick = (
        lax.broadcasted_iota(jnp.int32, (8, 1024), 1) // 128
        == lax.broadcasted_iota(jnp.int32, (8, 1024), 0)
    ).astype(BF)
    for chunk in range(4):
        cols = slice(chunk * 1024, (chunk + 1) * 1024)
        product = gown[:, cols].astype(F32) * oown[:, cols].astype(F32)
        high = product.astype(BF)
        low = (product - high.astype(F32)).astype(BF)
        deltas[chunk] = dot(pick, high, 1, 1) + dot(pick, low, 1, 1)
    for g in range(2):
        send(deltas.at[oc * 2 + g], deltas.at[4 + 2 * c + g], sib_s.at[4 + g], sib_r.at[4 + g], sibling, True)

    c_x.wait()
    c_wd.wait()
    total = jnp.zeros((128, 192), F32)
    for chunk in range(4):
        cols = slice(chunk * 2048, (chunk + 1) * 2048)
        total += dot(xv[:, cols], wd[:, cols], 1, 1)
    down_act[my_rows, :] = total.astype(BF)
    send(down_act.at[my_rows], down_act.at[my_rows], sib_s.at[6], sib_r.at[6], sibling, True)
    for d in range(NX):
        for cc in ([oc] if d == 0 else [0, 1]):
            xx = (x + d) % NX
            send(x_in.at[0, :, part(xx * 2 + cc, 1024, 1024)],
                 xcols.at[part(x * 2 + c, 128, 128)],
                 x_s.at[0], x_r.at[0], at(xx, y, z, cc))

    c_q.wait()
    c_g.wait()
    other_rows = part(oc, 128, 128)

    def heads_of(ref, g):
        return jnp.concatenate(
            [ref[:, part(g * 8 + h, 128, 128)] for h in range(8)], axis=0
        )

    sib_rows = part(y * 2 + oc, 128, 128)
    for g in range(2):
        c_kv[g][0].wait()
        c_kv[g][1].wait()

    def scores_of(g, j, first):
        rows = part(j, 256, 256)
        s = dot(kb[g, rows, :], heads_of(qb, g), 1, 1)
        if first:
            key_at = lax.broadcasted_iota(jnp.int32, (256, ROWS), 0)
            query_at = lax.broadcasted_iota(jnp.int32, (256, ROWS), 1) % 256
            s = jnp.where(key_at <= query_at, s, -jnp.inf)
        scores[g, rows, :] = s
        top = jnp.max(s, axis=0, keepdims=True)
        row_max[g] = top if first else jnp.maximum(row_max[g], top)

    def own_scores(g, carry):
        arrived(qb.at[other_rows, span_of(g)], sib_r.at[g])
        arrived(kb.at[g, sib_rows], kv_r.at[g, 0, y])
        scores_of(g, y, True)
        return carry

    lax.fori_loop(0, 2, own_scores, 0)

    def all_weights(g):
        def more_scores(t, inner):
            j = y - 1 - t
            arrived(kb.at[g, part(j, 256, 256)], kv_r.at[g, 0, j])
            scores_of(g, j, False)
            return inner

        lax.fori_loop(0, y, more_scores, 0)
        row_max[g] = row_max[g] * LOG2_SCALE

        def weights_of(j, sums):
            rows = part(j, 256, 256)
            found = []
            for h in range(0, 8, 2):
                qs = slice(h * 256, h * 256 + 512)
                w = jnp.exp2(scores[g, rows, qs] * LOG2_SCALE - row_max[g, :, qs])
                scores[g, rows, qs] = w
                found.append(jnp.sum(w, axis=0, keepdims=True))
            return sums + jnp.concatenate(found, axis=1)

        sums = lax.fori_loop(0, y + 1, weights_of, jnp.zeros((1, 2048), F32))
        row_max[g] = 1.0 / sums
        dq_acc[g] = jnp.zeros((128, 2048), F32)

    def grads_of(g, j):
        rows = part(j, 256, 256)
        keys, values = kb[g, rows, :], vb[g, rows, :]
        grad, query = heads_of(gb, g), heads_of(qb, g)
        prob_grad = dot(values, grad, 1, 1)
        prob = scores[g, rows, :] * row_max[g]
        score_grad = (prob * (prob_grad - delta_rows[g])).astype(BF)
        value_sum = dot(prob.astype(BF), grad, 1, 0)
        key_sum = dot(score_grad, query, 1, 0)
        dq_acc[g] = dq_acc[g] + dot(keys.T, score_grad, 1, 0)
        return key_sum * SCALE, value_sum

    def grads_copy(g, j):
        return remote(
            grads_out.at[g, j], grads_in.at[g, y], gr_s.at[j], gr_r.at[y], at(x, j, z, c)
        )

    def other_grads(g, carry):
        all_weights(g)
        arrived(gb.at[other_rows, span_of(g)], sib_r.at[2 + g])
        arrived(deltas.at[4 + 2 * oc + g], sib_r.at[4 + g])
        arrived(vb.at[g, sib_rows], kv_r.at[g, 1, y])
        mine = deltas[2 * c + g]
        theirs = deltas[4 + 2 * oc + g]
        low_half = jnp.where(c == 0, mine, theirs)
        high_half = jnp.where(c == 0, theirs, mine)
        for h in range(8):
            delta_rows[g, :, h * 256:h * 256 + 128] = low_half[h:h + 1]
            delta_rows[g, :, h * 256 + 128:(h + 1) * 256] = high_half[h:h + 1]

        def far_grads(t, inner):
            j = jnp.where(t == 0, jnp.maximum(y - 2, 0), jnp.where(t == y - 1, y - 1, t - 1))
            arrived(vb.at[g, part(j, 256, 256)], kv_r.at[g, 1, j])
            key_sum, value_sum = grads_of(g, j)
            grads_out[g, j, 0] = key_sum.astype(BF)
            grads_out[g, j, 1] = value_sum.astype(BF)
            grads_copy(g, j).start()
            return inner

        lax.fori_loop(0, y, far_grads, 0)
        return carry

    lax.fori_loop(0, 2, other_grads, 0)

    def last_grads(g, carry):
        key_sum, value_sum = grads_of(g, y)
        own_grads[g, 0] = key_sum
        own_grads[g, 1] = value_sum
        return carry

    lax.fori_loop(0, 2, last_grads, 0)
    for g in range(2):
        for h in range(8):
            first = (g * 8 + h) * 128
            dq_rows[:, first:first + 128] = (
                dq_acc[g, :, h * 256:(h + 1) * 256].T * SCALE
            ).astype(BF)

    arrived(down_act.at[other_rows], sib_r.at[6])

    def put_tiles(term, first):
        for k in range(NY):
            for t in range(term.shape[1] // 128):
                up_part[k, first + t] = term[k * 16:(k + 1) * 16, t * 128:(t + 1) * 128]

    def send_group(e):
        tiles = pl.ds(e * 5, 5)
        for d in range(1, NY):
            yy = (y + d) % NY
            send(up_part.at[yy, tiles], up_y.at[y, tiles], uy_s.at[0], uy_r.at[e],
                 at(x, yy, z, c))

    put_tiles(dot(down_act[:, 0:64], dq_rows[...], 0, 0).astype(BF), 0)
    for e in range(3):
        send_group(e)
    c_wq.wait()
    mid_part[:, 0:64] = dot(dq_rows[...], wq[...], 1, 1)

    c_wk.wait()
    c_wv.wait()
    def add_later(yy):
        arrived(grads_in.at[:, yy], gr_r.at[yy])
        for g in range(2):
            for which in range(2):
                own_grads[g, which] = own_grads[g, which] + grads_in[g, yy, which].astype(F32)

    each_later(add_later)
    for g in range(2):
        for which in range(2):
            kv_rows[which, :, g * 128:(g + 1) * 128] = own_grads[g, which].astype(BF)
    for which in range(2):
        weight = (wk, wv)[which]
        mid_part[:, 64 + 64 * which:128 + 64 * which] = dot(kv_rows[which], weight[...], 1, 1)
    send(mid_part, mid_sib, sib_s.at[11], sib_r.at[11], sibling, True)
    for which in range(2):
        act = down_act[:, 64 + 64 * which:128 + 64 * which]
        put_tiles(dot(act, kv_rows[which], 0, 0).astype(BF), 16 + 2 * which)
    send_group(3)

    arrived(mid_sib, sib_r.at[11])
    mid_all[part(x, 256, 256), :] = (mid_part[...] + mid_sib[...]).astype(BF)
    mid_rows = part(x * 2 + c, 128, 128)
    for d in range(1, NX):
        xx = (x + d) % NX
        send(mid_all.at[mid_rows], mid_all.at[mid_rows], mid_s.at[0], mid_r.at[x], at(xx, y, z, c))

    for g in range(2):
        span = slice(g * 1024, (g + 1) * 1024)
        there = part(c * 2 + g, 1024, 1024)
        local(dq_rows.at[my_rows, span], dq_out.at[0, :, there], 14 + g)
        send(dq_rows.at[other_rows, span], dq_out.at[0, :, there], sib_s.at[7 + g], sib_r.at[7 + g], sibling, True)
    there = part(c, 256, 256)
    for which, out in ((0, dk_out), (1, dv_out)):
        local(kv_rows.at[which, my_rows], out.at[0, :, there], 16 + which)
        send(kv_rows.at[which, other_rows], out.at[0, :, there],
             sib_s.at[9 + which], sib_r.at[9 + which], sibling, True)

    def owner_of(k):
        return (k // 5) * NZ + k % 5

    def to_owner(k):
        return remote(
            up_sum.at[k], up_rs.at[dp], us_s.at[0], us_r.at[0], {"dp": owner_of(k), "seq": seq}
        )

    def send_tile(k, carry):
        @pl.when(owner_of(k) != dp)
        def _():
            to_owner(k).start()
        return carry

    for e in range(4):
        tiles = pl.ds(e * 5, 5)
        up_y[y, tiles] = up_part[y, tiles]
        arrived(up_y.at[0:NY - 1, tiles], uy_r.at[e])
        first, second = up_y[0, tiles].astype(F32), up_y[1, tiles].astype(F32)
        third, fourth = up_y[2, tiles].astype(F32), up_y[3, tiles].astype(F32)
        up_sum[tiles] = ((first + second) + (third + fourth)).astype(BF)
        lax.fori_loop(e * 5, e * 5 + 5, send_tile, 0)

    own_tile = x * 5 + z
    owns = z < 5

    def final_copy(d):
        other = (dp + d) % (NX * NZ)
        return remote(
            up_fin.at[own_tile], up_fin.at[own_tile], ag_s.at[0], ag_r.at[x],
            {"dp": other, "seq": seq},
        )

    @pl.when(owns)
    def _():
        up_rs[dp] = up_sum[own_tile]

        arrived(up_rs.at[0:NX * NZ - 1], us_r.at[0])
        tile = jnp.sum(up_rs[...].astype(F32), axis=0)
        up_fin[own_tile] = (tile * FACTOR).astype(BF)

        def send_one(d, carry):
            final_copy(d).start()
            return carry

        lax.fori_loop(1, NX * NZ, send_one, 0)

    c_xc.wait()
    for d in range(1, NX):
        xx = (x + d) % NX
        rows = part(xx * 2 + c, 128, 128)
        arrived(mid_all.at[rows], mid_r.at[xx])
        send(mid_all.at[rows], mid_all.at[rows], fwd_s.at[0], fwd_r.at[0], sibling)
    arrived(xcols.at[0:128 * (2 * NX - 1)], x_r.at[0])
    arrived(mid_all.at[0:128 * (NX - 1)], fwd_r.at[0])
    mids = mid_all[...]
    for p in range(2):
        blocks = [
            dot(mids, xcols[:, zz * 256:(zz + 1) * 256], 0, 0) for zz in (2 * p, 2 * p + 1)
        ]
        packed = [found[0:128].T for found in blocks]
        packed.append(jnp.concatenate([found[128:192] for found in blocks], axis=0).T)
        for yy in range(NY):
            for k in range(3):
                down_part[yy, p, k] = packed[k][yy * 64:(yy + 1) * 64, :].astype(BF)
        for d in range(1, NY):
            yy = (y + d) % NY
            send(down_part.at[yy, p], down_y.at[y, p], dy_s.at[0], dy_r.at[p], at(x, yy, z, c))

    def down_copy(k, cc):
        return remote(
            down_z.at[k, cc * 32:(cc + 1) * 32], down_zin.at[z], dz_s.at[0], dz_r.at[0],
            at(x, y, 4 * c + k, cc),
        )

    for k in range(4):
        tiles = pl.ds(k * 5, 5)
        mine = jnp.logical_and(x == k, owns)

        @pl.when(mine)
        def _():
            arrived(up_fin.at[0:4], ag_r.at[k])

        @pl.when(jnp.logical_not(mine))
        def _():
            arrived(up_fin.at[0:5], ag_r.at[k])

        for d in range(1, NY):
            yy = (y + d) % NY
            send(up_fin.at[tiles], up_out.at[c, y, tiles], ay_s.at[0], ay_r.at[k],
                 at(x, yy, z, c))
        local(up_fin.at[tiles], up_out.at[c, y, tiles], 18 + k)
        send(up_fin.at[tiles], up_out.at[c, y, tiles], sh_s.at[0], sh_r.at[0], sibling)

    for k in range(4):
        if k % 2 == 0:
            p = k // 2
            down_y[y, p] = down_part[y, p]
            arrived(down_y.at[0:NY - 1, p], dy_r.at[p])
            first, second = down_y[0, p].astype(F32), down_y[1, p].astype(F32)
            third, fourth = down_y[2, p].astype(F32), down_y[3, p].astype(F32)
            summed = (first + second) + (third + fourth)
            for i in range(2):
                down_z[k + i] = jnp.concatenate(
                    [summed[i], summed[2][:, i * 64:(i + 1) * 64]], axis=1
                ).astype(BF)
        for cc in range(2):
            @pl.when(jnp.logical_or(4 * c + k != z, cc != c))
            def _():
                down_copy(k, cc).start()

    source_core = z // 4

    @pl.when(source_core == c)
    def _():
        down_zin[z] = down_z[z % 4, part(c, 32, 32), :]

    @pl.when(source_core == c)
    def _():
        arrived(down_zin.at[0:NZ - 1], dz_r.at[0])

    @pl.when(source_core != c)
    def _():
        arrived(down_zin, dz_r.at[0])

    down_sum[...] = jnp.sum(down_zin[...].astype(F32), axis=0) * FACTOR
    local(down_sum, down_out, 22)

    for e in range(4):
        tiles = pl.ds(e * 5, 5)
        arrived(up_out.at[c, 0:NY - 1, tiles], ay_r.at[e])
        for d in range(1, NY):
            yy = (y + d) % NY
            send(up_out.at[c, yy, tiles], up_out.at[c, yy, tiles], sh_s.at[0], sh_r.at[0], sibling)

    for copy in locals_[14:]:
        copy.wait()
    for g in range(2):
        there = part(oc * 2 + g, 1024, 1024)
        arrived(dq_out.at[0, :, there], sib_r.at[7 + g])
    there = part(oc, 256, 256)
    arrived(dk_out.at[0, :, there], sib_r.at[9])
    arrived(dv_out.at[0, :, there], sib_r.at[10])
    for copy in started:
        copy.wait_send()
    left(kb.at[:, 0:256], kv_s.at[y])

    def sent_later(yy):
        left(kb.at[:, 0:512], kv_s.at[yy])

    each_later(sent_later)

    def grads_sent(j, carry):
        left(grads_out.at[:, j], gr_s.at[j])
        return carry

    lax.fori_loop(0, y, grads_sent, 0)
    left(xcols.at[0:128 * (2 * NX - 1)], x_s.at[0])
    left(mid_all.at[0:128 * (NX - 1)], mid_s.at[0])
    left(mid_all.at[0:128 * (NX - 1)], fwd_s.at[0])
    left(down_part.at[0:NY - 1], dy_s.at[0])
    left(up_part.at[0:NY - 1], uy_s.at[0])
    left(up_out.at[c, 0:NY - 1], ay_s.at[0])
    left(up_out.at[c], sh_s.at[0])

    @pl.when(owns)
    def _():
        left(up_sum.at[0:19], us_s.at[0])
        left(up_rs.at[0:NX * NZ - 1], ag_s.at[0])

    @pl.when(jnp.logical_not(owns))
    def _():
        left(up_sum, us_s.at[0])

    @pl.when(source_core == c)
    def _():
        left(down_zin.at[0:NZ - 1], dz_s.at[0])

    @pl.when(source_core != c)
    def _():
        left(down_zin, dz_s.at[0])

    arrived(up_out.at[oc], sh_r.at[0])


def finish(
    dq_in, dk_in, dv_in, down_in, up_in, dq, dk, dv, down, upq, upk, upv,
    dq_v, dk_v, dv_v, down_v, up_v, upq_v, upk_v, upv_v, in_s, out_s,
):
    ins = [pltpu.make_async_copy(up_in, up_v, in_s.at[0])]
    outs = []
    for k in range(4):
        cols = pl.ds(k * 1024, 1024)
        ins.append(
            pltpu.make_async_copy(dq_in.at[:, :, cols], dq_v.at[:, :, cols], in_s.at[1 + k])
        )
        outs.append(pltpu.make_async_copy(dq_v.at[:, :, cols], dq.at[:, :, cols], out_s.at[k]))
    for k, (src, mid, dst) in enumerate(
        ((dk_in, dk_v, dk), (dv_in, dv_v, dv), (down_in, down_v, down))
    ):
        ins.append(pltpu.make_async_copy(src, mid, in_s.at[5 + k]))
        outs.append(pltpu.make_async_copy(mid, dst, out_s.at[4 + k]))
    ups = [
        pltpu.make_async_copy(
            upq_v.at[pl.ds(k * 16, 16)], upq.at[pl.ds(k * 16, 16)], out_s.at[7 + k]
        )
        for k in range(NY)
    ]
    ups += [
        pltpu.make_async_copy(upk_v, upk, out_s.at[11]),
        pltpu.make_async_copy(upv_v, upv, out_s.at[12]),
    ]
    for copy in ins:
        copy.start()
    for arriving, leaving in zip(ins[1:], outs):
        arriving.wait()
        leaving.start()
    ins[0].wait()
    for k in range(NY):
        rows = slice(k * 16, (k + 1) * 16)
        for cc in range(2):
            for t in range(20):
                tile = up_v[cc, k, t].astype(F32)
                if t < 16:
                    upq_v[rows, cc * 2048 + t * 128:cc * 2048 + (t + 1) * 128] = tile
                else:
                    first = cc * 256 + (t % 2) * 128
                    (upk_v if t < 18 else upv_v)[rows, first:first + 128] = tile
        ups[k].start()
    for copy in ups[4:]:
        copy.start()
    for copy in outs + ups:
        copy.wait()


def body(x_in, q_in, k_in, v_in, o_in, g_in, wd, wq, wk, wv):
    vm = pltpu.VMEM
    dma = pltpu.SemaphoreType.DMA
    any_ = pl.BlockSpec(memory_space=pl.ANY)
    shape = jax.ShapeDtypeStruct
    scratch = [
        vm((128, 8192), BF), vm((192, 8192), BF), vm((64, 2048), BF), vm((64, 256), BF),
        vm((64, 256), BF), vm((256, 2048), BF), vm((256, 2048), BF), vm((2, 1024, 128), BF),
        vm((2, 1024, 128), BF), vm((128, 4096), BF), vm((128, 4096), BF), vm((8, 8, 128), F32),
        vm((256, 192), BF),
        vm((1024, 1024), BF), vm((2, 1024, 2048), F32), vm((2, 1, 2048), F32),
        vm((2, 1, 2048), F32),
        vm((2, 128, 2048), F32),
        vm((256, 2048), BF), vm((2, 4, 2, 256, 128), BF), vm((2, 4, 2, 256, 128), BF),
        vm((2, 2, 256, 128), F32),
        vm((2, 256, 256), BF), vm((256, 192), F32), vm((256, 192), F32), vm((1024, 192), BF),
        vm((4, 2, 3, 64, 128), BF), vm((4, 2, 3, 64, 128), BF), vm((4, 64, 192), BF), vm((8, 32, 192), BF),
        vm((32, 192), F32),
        vm((4, 20, 16, 128), BF), vm((4, 20, 16, 128), BF), vm((20, 16, 128), BF),
        vm((32, 16, 128), BF), vm((20, 16, 128), BF),
        dma((23,)), dma((12,)), dma((12,)), dma((4,)), dma((2, 2, 4)), dma((1,)), dma((1,)),
        dma((4,)), dma((4,)), dma((1,)), dma((4,)), dma((1,)), dma((1,)),
        dma((1,)), dma((4,)), dma((1,)), dma((1,)), dma((1,)), dma((4,)), dma((1,)), dma((1,)),
        dma((1,)), dma((4,)), dma((1,)), dma((4,)), dma((1,)), dma((1,)),
    ]
    first = pl.pallas_call(
        kernel,
        out_shape=[
            shape((1, 128, 4096), BF), shape((1, 128, 512), BF), shape((1, 128, 512), BF),
            shape((32, 192), F32), shape((2, 4, 20, 16, 128), BF),
        ],
        in_specs=[any_] * 10,
        out_specs=[any_] * 5,
        scratch_shapes=scratch,
        compiler_params=pltpu.CompilerParams(
            vmem_limit_bytes=60 * 2**20, collective_id=0, has_side_effects=True
        ),
        cost_estimate=pl.CostEstimate(
            flops=8 * 10**9, bytes_accessed=12 * 2**20, transcendentals=4 * 2**20
        ),
    )(x_in, q_in, k_in, v_in, o_in, g_in, wd.T, wq, wk, wv)
    return pl.pallas_call(
        finish,
        out_shape=[
            shape((1, 128, 4096), BF), shape((1, 128, 512), BF), shape((1, 128, 512), BF),
            shape((32, 192), F32), shape((64, 4096), F32), shape((64, 512), F32),
            shape((64, 512), F32),
        ],
        in_specs=[any_] * 5,
        out_specs=[any_] * 7,
        scratch_shapes=[
            vm((1, 128, 4096), BF), vm((1, 128, 512), BF), vm((1, 128, 512), BF),
            vm((32, 192), F32), vm((2, 4, 20, 16, 128), BF), vm((64, 4096), F32),
            vm((64, 512), F32), vm((64, 512), F32), dma((8,)), dma((13,)),
        ],
        compiler_params=pltpu.CompilerParams(vmem_limit_bytes=60 * 2**20),
        cost_estimate=pl.CostEstimate(flops=10**6, bytes_accessed=6 * 2**20, transcendentals=0),
    )(*first)


def solution(mesh):
    token = P("dp", "seq", None)
    return jax.shard_map(
        body,
        mesh=mesh,
        in_specs=(token,) * 6 + (P(),) * 4,
        out_specs=(token,) * 3 + (P(("dp", "seq"), None), P(), P(), P()),
        check_vma=False,
    )
```
